256 devices in a mesh: ja: 16 (over y_hi, z), ka: 16 (over x, y_lo, core).
Axes of the slice: x: 4, y: 4 (y_hi: 2, y_lo: 2; y = y_hi * 2 + y_lo), z: 8, core: 2. Of those that a mesh axis runs over, the one named last changes fastest.
Arguments:
- pair_map: float32 [1536, 1536, 128], P('ja', 'ka'), may hold values from -45 to 45
- slab_rows: float32 [128, 1536, 128], P('ja', 'ka'), may hold values from -45 to 45
- norm_gain: float32 [128], replicated, may hold values from 0.1 to 1.9
- left_gate: float32 [128, 128], replicated, may hold values from -0.5 to 0.5
- left_value: float32 [128, 128], replicated, may hold values from -0.5 to 0.5
- right_gate: float32 [128, 128], replicated, may hold values from -0.5 to 0.5
- right_value: float32 [128, 128], replicated, may hold values from -0.5 to 0.5
- out_gain: float32 [128], replicated, may hold values from 0.1 to 1.9
- out_weight: float32 [128, 128], replicated, may hold values from -0.5 to 0.5
- cotangent: float32 [128, 1536, 128], P('ka', 'ja'), may hold values from -6 to 6
Outputs:
- update: float32 [128, 1536, 128], P('ka', 'ja')
- grad_pair: float32 [1536, 1536, 128], P('ja', 'ka')
- grad_slab: float32 [128, 1536, 128], P('ja', 'ka')
The draws below stay inside these ranges and needn't reach their ends.
All inputs are finite; a program needn't handle non-finite values.
Results may differ from the reference program's by a relative error of at most 0.0003.
Values sent between devices are 32-bit elements; how exact they have to be, the bound alone decides.
A program may use at most 192 MiB of HBM per device.

```python
import math
import jax
import jax.numpy as jnp
from jax import lax

C = 128
H = 128
N = 1536
I = 128


def spread_scales(key, rows, cols, width):
    first, second = jax.random.split(key)
    channel = jnp.exp(jax.random.uniform(first, (width,), jnp.float32, math.log(0.3), math.log(3.0)))
    cell = jnp.exp(jax.random.uniform(second, (rows, cols, 1), jnp.float32, math.log(0.3), math.log(3.0)))
    return channel * cell


def draw_pair_map(key, part):
    key = jax.random.fold_in(key, 11)
    first, second = jax.random.split(key)
    base = jax.random.truncated_normal(first, -5.0, 5.0, (N, N, C), jnp.float32)
    return base * spread_scales(second, N, N, C)


def draw_slab_rows(key, part):
    key = jax.random.fold_in(key, 12)
    first, second = jax.random.split(key)
    base = jax.random.truncated_normal(first, -5.0, 5.0, (I, N, C), jnp.float32)
    return base * spread_scales(second, I, N, C)


def shard_levels(stream_key, shape, cuts, low, high):
    loudness = 1.0
    for axis_at, parts in cuts:
        draws = jax.random.uniform(jax.random.fold_in(jax.random.fold_in(stream_key, 6), axis_at), (parts,), jnp.float32, low / len(cuts), high / len(cuts))
        loudness = loudness * jnp.repeat(jnp.exp(draws), shape[axis_at] // parts).reshape((-1,) + (1,) * (len(shape) - 1 - axis_at))
    return loudness


def centred(key, shape, deviation, reach, shards=(), kind=jnp.bfloat16):
    values = jax.random.normal(key, shape, jnp.float32) * deviation
    if len(shards) > 0:
        values = shard_levels(key, shape, shards, -0.22, 0.18) * values
    return jnp.clip(values, min=-reach, max=reach).astype(kind)


def setup_inputs(seed: int = 0) -> dict:
    keys = jax.random.split(jax.random.key(seed), 11)
    return {
        "pair_map": draw_pair_map(jax.random.fold_in(keys[10], 71), 0),
        "slab_rows": draw_slab_rows(jax.random.fold_in(keys[10], 71), 0),
        "norm_gain": jnp.clip(1.0 + 0.18 * jax.random.normal(keys[2], (C,), jnp.float32), 0.1, 1.9),
        "left_gate": centred(keys[3], (C, H), C ** -0.5, 0.5, (), jnp.float32),
        "left_value": centred(keys[4], (C, H), C ** -0.5, 0.5, (), jnp.float32),
        "right_gate": centred(keys[5], (C, H), C ** -0.5, 0.5, (), jnp.float32),
        "right_value": centred(keys[6], (C, H), C ** -0.5, 0.5, (), jnp.float32),
        "out_gain": jnp.clip(1.0 + 0.18 * jax.random.normal(keys[7], (H,), jnp.float32), 0.1, 1.9),
        "out_weight": centred(keys[8], (H, C), H ** -0.5, 0.5, (), jnp.float32),
        "cotangent": centred(keys[9], (I, N, C), 1.0, 6.0, ((0, 16), (1, 16)), jnp.float32),
    }


norm_eps = 1e-05

def layer_norm(values, gain):
    center = values - lax.optimization_barrier(jnp.mean(values, axis=-1, keepdims=True))
    spread = lax.optimization_barrier(jnp.mean(center * center, axis=-1, keepdims=True))
    return center * lax.rsqrt(spread + norm_eps) * gain

def project(values, gain, w_gate, w_value):
    normed = layer_norm(values, gain)
    gate = jnp.dot(normed, w_gate, precision=lax.Precision.HIGHEST, preferred_element_type=jnp.float32)
    value = jnp.dot(normed, w_value, precision=lax.Precision.HIGHEST, preferred_element_type=jnp.float32)
    return jax.nn.sigmoid(gate) * value

def finish(product, out_gain, out_weight):
    normed = layer_norm(product, out_gain)
    return jnp.dot(normed, out_weight, precision=lax.Precision.HIGHEST, preferred_element_type=jnp.float32)

def reference(pair_map, slab_rows, norm_gain, left_gate, left_value, right_gate, right_value, out_gain, out_weight, cotangent):
    blocks = pair_map.reshape(N // 32, 32, N, C)

    def right_block(block):
        return project(block, norm_gain, right_gate, right_value)
    right_map = lax.map(right_block, blocks).reshape(N, N, H)
    left_map, back_left = jax.vjp(lambda slab: project(slab, norm_gain, left_gate, left_value), slab_rows)
    product = jnp.einsum('ikh,jkh->ijh', left_map, right_map, precision=lax.Precision.HIGHEST)
    update, back_out = jax.vjp(lambda prod_in: finish(prod_in, out_gain, out_weight), product)
    grad_product = back_out(cotangent)[0]
    grad_left = jnp.einsum('ijh,jkh->ikh', grad_product, right_map, precision=lax.Precision.HIGHEST)
    grad_right = jnp.einsum('ijh,ikh->jkh', grad_product, left_map, precision=lax.Precision.HIGHEST)
    grad_slab = back_left(grad_left)[0]

    def pull_block(pieces):
        block, grad_block = pieces
        back_block = jax.vjp(right_block, block)[1]
        return back_block(grad_block)[0]
    grad_pair = lax.map(pull_block, (blocks, grad_right.reshape(N // 32, 32, N, H))).reshape(N, N, C)
    return (update, grad_pair, grad_slab)
```

```python
import jax
import jax.numpy as jnp
from jax import lax
from jax.experimental import pallas as pl
from jax.experimental.pallas import tpu as pltpu
from jax.sharding import PartitionSpec as P

f32, bf16 = jnp.float32, jnp.bfloat16
norm_eps = 1e-05

YH, Z, X, YL, CORE = 2, 8, 4, 2, 2
C = 2
NR = 8 // C
HR, QR = NR // 2, NR // 4
CI = 16 * NR
B = 96
T = (B, 128)
MIB = 2**20
MESH = pl.DeviceIdType.MESH
NT = (((1,), (1,)), ((), ()))
NN = (((1,), (0,)), ((), ()))
VM = pl.BlockSpec(memory_space=pltpu.VMEM)
HBM = pl.BlockSpec(memory_space=pl.ANY)


def split(values):
    hi = values.astype(bf16)
    return hi, (values - hi.astype(f32)).astype(bf16)


def dot(a, b, dims=NN):
    return lax.dot_general(a, b, dims, preferred_element_type=f32)


def dot3(a, b, dims=NN):
    a_hi, a_lo = split(a)
    b_hi, b_lo = split(b)
    both = dot(jnp.concatenate([a_hi, a_lo], 1), jnp.concatenate([b_hi, b_hi], dims[0][1][0]), dims)
    return both + dot(a_hi, b_lo, dims)


def mean(values):
    return jnp.mean(values, axis=-1, keepdims=True)


def normalise(values):
    center = values - mean(values)
    scale = lax.rsqrt(mean(center * center) + norm_eps)
    return center * scale, scale


def prepare(gain_col, gate, value, w_up, w_low, wc_hi, wc_lo):
    folded = jnp.concatenate([gate[...] * gain_col[...], value[...] * gain_col[...]], 1)
    hi, lo = split(folded)
    w_up[:128] = hi
    w_up[128:] = hi
    w_low[...] = lo
    if wc_hi is not None:
        hi, lo = split(folded - jnp.mean(folded, axis=0, keepdims=True))
        wc_hi[...] = hi
        wc_lo[...] = lo


def gates(normed, w_up, w_low):
    hi, lo = split(normed)
    both = dot(jnp.concatenate([hi, lo], 1), w_up[...]) + dot(hi, w_low[...])
    return 1.0 / (1.0 + jnp.exp(-both[:, :128])), both[:, 128:]


def forward(values, w_up, w_low):
    s, v = gates(normalise(values)[0], w_up, w_low)
    return s * v


def pull(values, grad, w_up, w_low, wc_hi, wc_lo):
    normed, scale = normalise(values)
    s, v = gates(normed, w_up, w_low)
    d_value = grad * s
    d_gate = d_value * v * (1.0 - s)
    hi, lo = split(jnp.concatenate([d_gate, d_value], 1))
    d = dot(hi, wc_hi[...], NT) + dot(lo, wc_hi[...], NT) + dot(hi, wc_lo[...], NT)
    return scale * (d - normed * mean(d * normed))


def accumulate(dst, src):
    dims = src.shape[:-2]
    if not dims:
        dst[...] = dst[...] + src[...]
        return

    def step(i, _):
        accumulate(dst.at[i], src.at[i])
        return 0

    lax.fori_loop(0, dims[0], step, 0, unroll=True)


def repeat(n, body):
    def step(i, _):
        body(i)
        return 0

    lax.fori_loop(0, n, step, 0, unroll=True)


def run(n, body, events=()):
    def step(t, _):
        for at, event in events:
            pl.when(t == at)(event)
        body(t)
        return 0

    lax.fori_loop(0, n, step, 0)


def rows_in(src, dst, first, n):
    flat = dst.reshape(dst.shape[0] * dst.shape[1], 128)

    def body(u):
        row = first + u
        tile = jnp.concatenate([src[row], jnp.zeros((32, 128), f32)], 0).T
        flat[pl.ds(row, 128, stride=dst.shape[1]), :] = tile

    repeat(n, body)


def rows_out(src, dst, first, n):
    flat = src.reshape(src.shape[0] * src.shape[1], 128)

    def body(u):
        row = first + u
        dst[row] = flat[pl.ds(row, 128, stride=src.shape[1]), :].T[:B]

    repeat(n, body)


class Net:
    def __init__(self, ss, rs):
        self.ss, self.rs = ss, rs
        self.keys, self.sent = {}, []
        ja, ka = lax.axis_index("ja"), lax.axis_index("ka")
        self.yh, self.z = ja // 8, ja % 8
        self.x, self.yl, self.cc = ka // 4, (ka // 2) % 2, ka % 2
        self.yh1, self.yl1, self.cc1 = 1 - self.yh, 1 - self.yl, 1 - self.cc
        self.zs = {d: (self.z + d + 8) % 8 for d in range(-4, 5)}
        self.xs = {d: (self.x + d + 4) % 4 for d in range(-2, 3)}
        self.to = {
            "z+": (self.yh * 8 + self.zs[1], ka),
            "z-": (self.yh * 8 + self.zs[-1], ka),
            "yh": (self.yh1 * 8 + self.z, ka),
            "x+": (ja, self.xs[1] * 4 + ka % 4),
            "x-": (ja, self.xs[-1] * 4 + ka % 4),
            "yl": (ja, self.x * 4 + self.yl1 * 2 + self.cc),
            "cc": (ja, self.x * 4 + self.yl * 2 + self.cc1),
        }

    def greet(self):
        barrier = pltpu.get_barrier_semaphore()
        for dev in self.to.values():
            pl.semaphore_signal(barrier, inc=1, device_id=dev, device_id_type=MESH)
        return lambda: pl.semaphore_wait(barrier, len(self.to))

    def copy(self, src, dst, key, way):
        k = self.keys.setdefault(key, len(self.keys))
        return pltpu.make_async_remote_copy(
            src_ref=src(),
            dst_ref=dst(),
            send_sem=self.ss.at[k],
            recv_sem=self.rs.at[k],
            device_id=self.to[way],
            device_id_type=MESH,
        )

    def send(self, src, dst, key, way):
        self.copy(src, dst, key, way).start()
        self.sent.append((src, dst, key, way))

    def recv(self, dst, key, way):
        self.copy(dst, dst, key, way).wait_recv()

    def drain(self):
        for entry in self.sent:
            self.copy(*entry).wait_send()


ways = ((0, 1, "+"), (1, -1, "-"))


class GatherJa:
    def __init__(self, net, W, c):
        self.n, self.W, self.c = net, W, c

    def at(self, yh, z, lo, hi):
        return lambda: self.W.at[self.c, yh, z, pl.ds(lo, hi - lo)]

    def part(self, stream, d, s):
        if stream == "own":
            return (0, NR) if s < 4 else ((0, HR), (HR, NR))[d]
        return (0, HR) if s < 4 else ((0, QR), (QR, HR))[d]

    def hop(self, stream, d, sign, s):
        n = self.n
        col = n.yh if stream == "own" else n.yh1
        ref = self.at(col, n.zs[-sign * (s - 1)], *self.part(stream, d, s))
        n.send(ref, ref, ("ag", self.c, stream, d, s), "z+" if d == 0 else "z-")

    def got(self, stream, d, sign, s):
        n = self.n
        col = n.yh if stream == "own" else n.yh1
        ref = self.at(col, n.zs[-sign * s], *self.part(stream, d, s))
        n.recv(ref, ("ag", self.c, stream, d, s), "z+" if d == 0 else "z-")

    def over(self, d, sign, s):
        ref = self.at(self.n.yh, self.n.zs[-sign * s], HR, NR)
        self.n.send(ref, ref, ("agy", self.c, d, s), "yh")

    def over_got(self, d, sign, s):
        ref = self.at(self.n.yh1, self.n.zs[-sign * s], HR, NR)
        self.n.recv(ref, ("agy", self.c, d, s), "yh")

    def start(self):
        for d, sign, _ in ways:
            self.hop("own", d, sign, 1)
        ref = self.at(self.n.yh, self.n.z, 0, NR)
        self.n.send(ref, ref, ("agy0", self.c), "yh")

    def start_a(self):
        ref = self.at(self.n.yh1, self.n.z, 0, NR)
        self.n.recv(ref, ("agy0", self.c), "yh")
        for d, sign, _ in ways:
            self.hop("a", d, sign, 1)

    def own(self, s):
        def event():
            for d, sign, _ in ways:
                self.got("own", d, sign, s)
                if s < 4:
                    self.hop("own", d, sign, s + 1)
                    self.over(d, sign, s)
                elif d == 1:
                    self.over(d, sign, s)

        return event

    def a(self, s):
        def event():
            for d, sign, _ in ways:
                self.got("a", d, sign, s)
                if s < 4:
                    self.hop("a", d, sign, s + 1)

        return event

    def finish(self):
        for s in range(1, 4):
            for d, sign, _ in ways:
                self.over_got(d, sign, s)
        self.over_got(1, -1, 4)


class ScatterKa:
    def __init__(self, net, Pn, Q, bufs, c):
        self.n, self.Pn, self.Q, self.c = net, Pn, Q, c
        self.x1a, self.x1b, self.y2, self.x2a, self.x2b, self.y1 = bufs

    def start(self):
        n, c = self.n, self.c
        n.send(lambda: self.Pn.at[c, :, :, n.cc1], lambda: self.Q.at[c], ("core", c), "cc")

    def q(self, x, yl, lo, hi):
        if yl is None:
            return lambda: self.Q.at[self.c, x, :, pl.ds(lo, hi - lo)]
        return lambda: self.Q.at[self.c, x, yl, pl.ds(lo, hi - lo)]

    def one(self):
        n, c = self.n, self.c
        n.recv(lambda: self.Q.at[c], ("core", c), "cc")
        accumulate(self.Q.at[c], self.Pn.at[c, :, :, n.cc])
        n.send(lambda: self.Q.at[c, :, n.yl1, pl.ds(HR, HR)], lambda: self.y2.at[c], ("y2", c), "yl")
        for d, sign, w in ways:
            n.send(self.q(n.xs[2], None, d * QR, d * QR + QR), lambda: self.x1a.at[c, d], ("x1a", c, d), "x" + w)

    def two(self):
        n, c = self.n, self.c
        for d, sign, w in ways:
            n.recv(lambda: self.x1a.at[c, d], ("x1a", c, d), "x" + w)
            accumulate(self.q(n.xs[sign], None, d * QR, d * QR + QR)(), self.x1a.at[c, d])
            n.send(self.q(n.xs[sign], None, 0, HR), lambda: self.x1b.at[c, d], ("x1b", c, d), "x" + w)

    def three(self):
        n, c = self.n, self.c
        n.recv(lambda: self.y2.at[c], ("y2", c), "yl")
        accumulate(self.Q.at[c, :, n.yl, pl.ds(HR, HR)], self.y2.at[c])
        for d, sign, w in ways:
            lo = HR + d * QR
            n.send(self.q(n.xs[2], n.yl, lo, lo + QR), lambda: self.x2a.at[c, d], ("x2a", c, d), "x" + w)

    def four(self):
        n, c = self.n, self.c
        for d, sign, w in ways:
            n.recv(lambda: self.x1b.at[c, d], ("x1b", c, d), "x" + w)
            accumulate(self.q(n.x, None, 0, HR)(), self.x1b.at[c, d])
        n.send(self.q(n.x, n.yl1, 0, HR), lambda: self.y1.at[c], ("y1", c), "yl")

    def five(self):
        n, c = self.n, self.c
        for d, sign, w in ways:
            lo = HR + d * QR
            n.recv(lambda: self.x2a.at[c, d], ("x2a", c, d), "x" + w)
            accumulate(self.q(n.xs[sign], n.yl, lo, lo + QR)(), self.x2a.at[c, d])
            n.send(self.q(n.xs[sign], n.yl, HR, NR), lambda: self.x2b.at[c, d], ("x2b", c, d), "x" + w)

    def six(self):
        n, c = self.n, self.c
        n.recv(lambda: self.y1.at[c], ("y1", c), "yl")
        accumulate(self.q(n.x, n.yl, 0, HR)(), self.y1.at[c])
        for d, sign, w in ways:
            n.recv(lambda: self.x2b.at[c, d], ("x2b", c, d), "x" + w)
            accumulate(self.q(n.x, n.yl, HR, NR)(), self.x2b.at[c, d])


class GatherKa:
    def __init__(self, net, G, c):
        self.n, self.G, self.c = net, G, c

    def g(self, x, yl, core, lo, hi):
        if yl is None:
            return lambda: self.G.at[self.c, x, :, core, pl.ds(lo, hi - lo)]
        return lambda: self.G.at[self.c, x, yl, core, pl.ds(lo, hi - lo)]

    def put(self, key, way, *where):
        ref = self.g(*where)
        self.n.send(ref, ref, ("agk", self.c) + key, way)

    def get(self, key, way, *where):
        self.n.recv(self.g(*where), ("agk", self.c) + key, way)

    def zero(self):
        n = self.n
        self.put(("y1",), "yl", n.x, n.yl, n.cc, 0, HR)
        for d, sign, w in ways:
            self.put(("x2", d), "x" + w, n.x, n.yl, n.cc, HR, NR)
        self.put(("c0",), "cc", n.x, n.yl, n.cc, 0, NR)
        self.put(("y2", 0), "yl", n.x, n.yl, n.cc, HR, NR)

    def one(self):
        n = self.n
        self.get(("y1",), "yl", n.x, n.yl1, n.cc, 0, HR)
        for d, sign, w in ways:
            self.put(("x1", d), "x" + w, n.x, None, n.cc, 0, HR)
        self.put(("c1",), "cc", n.x, n.yl1, n.cc, 0, HR)

    def two(self):
        n = self.n
        for d, sign, w in ways:
            src = n.xs[-sign]
            self.get(("x2", d), "x" + w, src, n.yl, n.cc, HR, NR)
            self.put(("x2h", d), "x" + w, src, n.yl, n.cc, HR + d * QR, HR + d * QR + QR)
            self.put(("y2", 1 + d), "yl", src, n.yl, n.cc, HR, NR)
            self.put(("c2", d), "cc", src, n.yl, n.cc, HR, NR)

    def three(self):
        n = self.n
        for d, sign, w in ways:
            src = n.xs[-sign]
            self.get(("x1", d), "x" + w, src, None, n.cc, 0, HR)
            self.put(("x1h", d), "x" + w, src, None, n.cc, d * QR, d * QR + QR)
            self.put(("c3", d), "cc", src, None, n.cc, 0, HR)

    def four(self):
        n = self.n
        for d, sign, w in ways:
            self.get(("x2h", d), "x" + w, n.xs[2], n.yl, n.cc, HR + d * QR, HR + d * QR + QR)
        self.put(("y2", 3), "yl", n.xs[2], n.yl, n.cc, HR, NR)
        self.put(("c4",), "cc", n.xs[2], n.yl, n.cc, HR, NR)
        for d, sign, w in ways:
            src = n.xs[-sign]
            self.get(("y2", 1 + d), "yl", src, n.yl1, n.cc, HR, NR)
            self.put(("c6", 1 + d), "cc", src, n.yl1, n.cc, HR, NR)
        self.get(("y2", 0), "yl", n.x, n.yl1, n.cc, HR, NR)
        self.put(("c6", 0), "cc", n.x, n.yl1, n.cc, HR, NR)

    def five(self):
        n = self.n
        for d, sign, w in ways:
            self.get(("x1h", d), "x" + w, n.xs[2], None, n.cc, d * QR, d * QR + QR)
        self.put(("c5",), "cc", n.xs[2], None, n.cc, 0, HR)
        self.get(("y2", 3), "yl", n.xs[2], n.yl1, n.cc, HR, NR)
        self.put(("c6", 3), "cc", n.xs[2], n.yl1, n.cc, HR, NR)

    def finish(self):
        n = self.n
        o = n.cc1
        self.get(("c0",), "cc", n.x, n.yl, o, 0, NR)
        self.get(("c1",), "cc", n.x, n.yl1, o, 0, HR)
        for d, sign, w in ways:
            src = n.xs[-sign]
            self.get(("c2", d), "cc", src, n.yl, o, HR, NR)
            self.get(("c3", d), "cc", src, None, o, 0, HR)
            self.get(("c6", 1 + d), "cc", src, n.yl1, o, HR, NR)
        self.get(("c4",), "cc", n.xs[2], n.yl, o, HR, NR)
        self.get(("c5",), "cc", n.xs[2], None, o, 0, HR)
        self.get(("c6", 0), "cc", n.x, n.yl1, o, HR, NR)
        self.get(("c6", 3), "cc", n.xs[2], n.yl1, o, HR, NR)


class ScatterJa:
    def __init__(self, net, N, bufs, c):
        self.n, self.N, self.c = net, N, c
        self.ry, self.ra1, self.ra, self.rb1, self.rb, self.rf = bufs

    def rows(self, stream, d, s):
        lo = 0 if stream == "a" else HR
        return (lo, lo + HR) if s > 1 else (lo + d * QR, lo + d * QR + QR)

    def block(self, stream, z, lo, hi):
        if stream == "a":
            return lambda: self.N.at[self.c, :, z, pl.ds(lo, hi - lo)]
        return lambda: self.N.at[self.c, self.n.yh, z, pl.ds(lo, hi - lo)]

    def land(self, stream, d, s):
        first, rest = (self.ra1, self.ra) if stream == "a" else (self.rb1, self.rb)
        if s == 1:
            return lambda: first.at[self.c, d]
        return lambda: rest.at[self.c, d, s - 2]

    def push(self, stream, d, sign, w, s):
        src = self.block(stream, self.n.zs[sign * (5 - s)], *self.rows(stream, d, s))
        self.n.send(src, self.land(stream, d, s), ("rs", self.c, stream, d, s), "z" + w)

    def take(self, stream, d, sign, w, s):
        land = self.land(stream, d, s)
        self.n.recv(land, ("rs", self.c, stream, d, s), "z" + w)
        dst = self.block(stream, self.n.zs[sign * (4 - s)], *self.rows(stream, d, s))
        accumulate(dst(), land())

    def start(self):
        n, c = self.n, self.c
        n.send(lambda: self.N.at[c, n.yh1, :, pl.ds(HR, HR)], lambda: self.ry.at[c], ("rsy", c), "yh")
        for d, sign, w in ways:
            self.push("a", d, sign, w, 1)

    def start_b(self):
        n, c = self.n, self.c
        n.recv(lambda: self.ry.at[c], ("rsy", c), "yh")
        accumulate(self.N.at[c, n.yh, :, pl.ds(HR, HR)], self.ry.at[c])
        for d, sign, w in ways:
            self.push("b", d, sign, w, 1)

    def step(self, stream, s):
        def event():
            for d, sign, w in ways:
                self.take(stream, d, sign, w, s)
                if s < 4:
                    self.push(stream, d, sign, w, s + 1)
            if s == 4 and stream == "a":
                self.n.send(
                    lambda: self.N.at[self.c, self.n.yh1, self.n.z, pl.ds(0, HR)],
                    lambda: self.rf.at[self.c],
                    ("rsf", self.c),
                    "yh",
                )

        return event

    def finish(self):
        n, c = self.n, self.c
        n.recv(lambda: self.rf.at[c], ("rsf", c), "yh")
        accumulate(N_at(self.N, c, n, 0, HR), self.rf.at[c])


def N_at(N, c, n, lo, hi):
    return N.at[c, n.yh, n.z, pl.ds(lo, hi - lo)]


def first_kernel(
    pair, slab, gain_col, left_gate, left_value, right_gate, right_value, out_gain, out_weight, cot,
    update, own_grad, right_out, left_out,
    xv, wl_up, wl_low, wr_up, wr_low, W, Rt, Lt, Hb, Pn, Q, x1a, x1b, y2, x2a, x2b, y1, ss, rs, local,
):
    net = Net(ss, rs)
    entered = net.greet()
    load = pltpu.make_async_copy(pair, xv, local.at[0])
    load.start()
    prepare(gain_col, left_gate, left_value, wl_up, wl_low, None, None)
    ag = [GatherJa(net, W, c) for c in range(C)]
    rk = [ScatterKa(net, Pn, Q, (x1a, x1b, y2, x2a, x2b, y1), c) for c in range(C)]

    for c in range(C):
        own = forward(slab[c * NR : (c + 1) * NR].reshape(NR * B, 128), wl_up, wl_low)
        W[c, net.yh, net.z] = own.reshape(NR, B, 128)
        if c == 0:
            entered()
            ag[0].start()
    prepare(gain_col, right_gate, right_value, wr_up, wr_low, None, None)
    load.wait()

    flat_R = Rt.reshape(128 * B, 128)

    def right_step(t):
        G = 4
        made = forward(xv[pl.ds(t * G, G)].reshape(G * B, 128), wr_up, wr_low)
        for u in range(G):
            tile = jnp.concatenate([made[u * B : (u + 1) * B], jnp.zeros((32, 128), f32)], 0).T
            flat_R[pl.ds(t * G + u, 128, stride=B), :] = tile

    a0 = ag[0]
    run(24, right_step, [(4, a0.start_a), (7, a0.own(1)), (9, a0.a(1)), (14, a0.own(2)), (16, a0.a(2)), (22, a0.own(3))])
    save_right = pltpu.make_async_copy(Rt, right_out, local.at[1])
    save_right.start()
    a0.a(3)()

    Wf = W.reshape(C * 16 * NR, B, 128)

    def turn_left(c, lo, hi, events=()):
        base = c * CI + lo
        run((hi - lo) // 8, lambda t: rows_in(Wf, Lt, base + t * 8, 8), events)

    def product(c, events=()):
        def body(t):
            def one(u):
                h = t * 8 + u
                Hb[h, c * CI : (c + 1) * CI, :B] = dot3(Lt[h, c * CI : (c + 1) * CI, :], Rt[h], NT)

            repeat(8, one)

        run(16, body, events)

    Pf = Pn.reshape(C * 16 * NR, B, 128)

    def turn_product(c, events=()):
        run(CI // 8, lambda t: rows_out(Hb, Pf, c * CI + t * 8, 8), events)

    def finish_rows(c):
        def body(u):
            r = c * NR + u
            normed, scale = normalise(Q[c, net.x, net.yl, u])
            update[r] = dot3(normed * out_gain[...], out_weight[...])
            d = dot3(cot[r], out_weight[...], NT) * out_gain[...]
            own_grad[r] = scale * (d - mean(d) - normed * mean(d * normed))

        run(NR, body)

    if C == 1:
        a0.own(4)()
        a0.a(4)()
        a0.finish()
        turn_left(0, 0, CI)
        product(0)
        turn_product(0)
    else:
        a1 = ag[1]
        a1.start()
        a0.own(4)()
        a0.a(4)()
        a0.finish()
        turn_left(0, 0, CI, [(2, a1.start_a)])
        a1.own(1)()
        product(0, [(3, a1.a(1)), (9, a1.own(2)), (13, a1.a(2))])
        turn_product(0)
        rk[0].start()
        a1.own(3)()
        rk[0].one()
        a1.a(3)()
        rk[0].two()
        rk[0].three()
        a1.own(4)()
        a1.a(4)()
        a1.finish()
        turn_left(1, 0, CI, [(3, rk[0].four), (6, rk[0].five)])
        product(1, [(6, rk[0].six)])
        turn_product(1)
    save_left = pltpu.make_async_copy(Lt, left_out, local.at[2])
    save_left.start()
    last = rk[C - 1]
    last.start()
    if C == 2:
        finish_rows(0)
    last.one()
    last.two()
    last.three()
    last.four()
    last.five()
    last.six()
    finish_rows(C - 1)
    net.drain()
    save_right.wait()
    save_left.wait()


def second_kernel(
    pair, slab, gain_col, left_gate, left_value, right_gate, right_value, own_grad, right_in, left_in,
    grad_pair, grad_slab,
    xv, wl_up, wl_low, wlc_hi, wlc_lo, wr_up, wr_low, wrc_hi, wrc_lo,
    Rt, Lt, G, Gt, Hb, N, ry, ra1, ra, rb1, rb, rf, ss, rs, local,
):
    net = Net(ss, rs)
    entered = net.greet()
    loads = [
        pltpu.make_async_copy(right_in, Rt, local.at[0]),
        pltpu.make_async_copy(left_in, Lt, local.at[1]),
        pltpu.make_async_copy(pair, xv, local.at[2]),
    ]
    for load in loads:
        load.start()
    gk = [GatherKa(net, G, c) for c in range(C)]
    sj = [ScatterJa(net, N, (ry, ra1, ra, rb1, rb, rf), c) for c in range(C)]
    for c in range(C):
        G[c, net.x, net.yl, net.cc] = own_grad[c * NR : (c + 1) * NR]
    entered()
    g0 = gk[0]
    g0.zero()
    prepare(gain_col, left_gate, left_value, wl_up, wl_low, wlc_hi, wlc_lo)
    prepare(gain_col, right_gate, right_value, wr_up, wr_low, wrc_hi, wrc_lo)
    g0.one()
    g0.two()
    g0.three()
    if C == 2:
        gk[1].zero()
    g0.four()
    g0.five()
    g0.finish()
    for load in loads:
        load.wait()

    Gf = G.reshape(C * 16 * NR, B, 128)
    Nf = N.reshape(C * 16 * NR, B, 128)

    def turn_grad(c, events=()):
        run(CI // 8, lambda t: rows_in(Gf, Gt, c * CI + t * 8, 8), events)

    def left_product(c, events=()):
        def body(t):
            def one(u):
                h = t * 8 + u
                right = jnp.concatenate([Rt[h], jnp.zeros((32, 128), f32)], 0)
                Hb[h, c * CI : (c + 1) * CI, :] = dot3(Gt[h, c * CI : (c + 1) * CI, :], right)

            repeat(8, one)

        run(16, body, events)

    def turn_back(c, events=()):
        run(CI // 8, lambda t: rows_out(Hb, Nf, c * CI + t * 8, 8), events)

    def right_product(events=()):
        def body(t):
            def one(u):
                h = t * 8 + u
                Hb[h, :B, :] = dot3(Gt[h].T, Lt[h])[:B]

            repeat(8, one)

        run(16, body, events)

    flat_H = Hb.reshape(128 * 128, 128)

    def right_pull(events=()):
        K = 4

        def body(t):
            grads = jnp.concatenate(
                [flat_H[pl.ds(t * K + u, 128, stride=128), :].T[:B] for u in range(K)], 0
            )
            out = pull(xv[pl.ds(t * K, K)].reshape(K * B, 128), grads, wr_up, wr_low, wrc_hi, wrc_lo)
            grad_pair[pl.ds(t * K, K)] = out.reshape(K, B, 128)

        run(24, body, events)

    def left_pull(c):
        grads = N[c, net.yh, net.z].reshape(NR * B, 128)
        out = pull(slab[c * NR : (c + 1) * NR].reshape(NR * B, 128), grads, wl_up, wl_low, wlc_hi, wlc_lo)
        grad_slab[c * NR : (c + 1) * NR] = out.reshape(NR, B, 128)

    if C == 1:
        turn_grad(0)
        left_product(0)
        turn_back(0)
        s = sj[0]
        s.start()
        right_product([(8, s.step("a", 1))])
        right_pull([(0, s.step("a", 2)), (8, s.step("a", 3)), (16, s.step("a", 4))])
        s.start_b()
        for k in range(1, 5):
            s.step("b", k)()
        s.finish()
        left_pull(0)
    else:
        g1 = gk[1]
        turn_grad(0, [(2, g1.one), (5, g1.two)])
        left_product(0, [(2, g1.three), (10, g1.four)])
        turn_back(0, [(4, g1.five)])
        s, e = sj
        s.start()
        g1.finish()
        turn_grad(1, [(4, s.step("a", 1))])
        left_product(1, [(4, s.step("a", 2)), (13, s.step("a", 3))])
        turn_back(1, [(3, s.start_b)])
        s.step("a", 4)()
        e.start()
        right_product(
            [(2, s.step("b", 1)), (5, s.step("b", 2)), (8, s.step("b", 3)), (11, e.step("a", 1)), (13, s.step("b", 4))]
        )
        right_pull(
            [(0, s.finish), (1, e.step("a", 2)), (7, e.step("a", 3)), (10, e.start_b), (13, e.step("a", 4)),
             (16, e.step("b", 1)), (19, e.step("b", 2)), (22, e.step("b", 3))]
        )
        left_pull(0)
        e.step("b", 4)()
        e.finish()
        left_pull(1)
    net.drain()


def shards(
    pair_map, slab_rows, norm_gain, left_gate, left_value, right_gate, right_value, out_gain, out_weight, cotangent
):
    S = jax.ShapeDtypeStruct
    V = pltpu.VMEM
    weights = [V((256, 256), bf16), V((128, 256), bf16)]
    gain_col = norm_gain.reshape(128, 1)
    update, own_grad, right_turned, left_turned = pl.pallas_call(
        first_kernel,
        out_shape=[S((8,) + T, f32), S((8,) + T, f32), S((128, B, 128), f32), S((128, 128, 128), f32)],
        in_specs=[HBM] + [VM] * 9,
        out_specs=[VM, VM, HBM, HBM],
        scratch_shapes=[V((B,) + T, f32)]
        + weights * 2
        + [
            V((C, YH, Z, NR) + T, f32),
            V((128, B, 128), f32),
            V((128, 128, 128), f32),
            V((128, 128, 128), f32),
            V((C, X, YL, CORE, NR) + T, f32),
            V((C, X, YL, NR) + T, f32),
            V((C, 2, YL, QR) + T, f32),
            V((C, 2, YL, HR) + T, f32),
            V((C, X, HR) + T, f32),
            V((C, 2, QR) + T, f32),
            V((C, 2, HR) + T, f32),
            V((C, HR) + T, f32),
            pltpu.SemaphoreType.DMA((80,)),
            pltpu.SemaphoreType.DMA((80,)),
            pltpu.SemaphoreType.DMA((3,)),
        ],
        compiler_params=pltpu.CompilerParams(collective_id=1, has_side_effects=True, vmem_limit_bytes=60 * MIB),
        name="first",
    )(
        pair_map, slab_rows, gain_col, left_gate, left_value, right_gate, right_value,
        out_gain.reshape(1, 128), out_weight, cotangent,
    )
    grad_pair, grad_slab = pl.pallas_call(
        second_kernel,
        out_shape=[S((B,) + T, f32), S((8,) + T, f32)],
        in_specs=[HBM] + [VM] * 7 + [HBM] * 2,
        out_specs=[VM, VM],
        scratch_shapes=[V((B,) + T, f32)]
        + (weights + [V((128, 256), bf16)] * 2) * 2
        + [
            V((128, B, 128), f32),
            V((128, 128, 128), f32),
            V((C, X, YL, CORE, NR) + T, f32),
            V((128, 128, 128), f32),
            V((128, 128, 128), f32),
            V((C, YH, Z, NR) + T, f32),
            V((C, Z, HR) + T, f32),
            V((C, 2, YH, QR) + T, f32),
            V((C, 2, 3, YH, HR) + T, f32),
            V((C, 2, QR) + T, f32),
            V((C, 2, 3, HR) + T, f32),
            V((C, HR) + T, f32),
            pltpu.SemaphoreType.DMA((96,)),
            pltpu.SemaphoreType.DMA((96,)),
            pltpu.SemaphoreType.DMA((3,)),
        ],
        compiler_params=pltpu.CompilerParams(collective_id=2, has_side_effects=True, vmem_limit_bytes=62 * MIB),
        name="second",
    )(pair_map, slab_rows, gain_col, left_gate, left_value, right_gate, right_value, own_grad, right_turned, left_turned)
    return (update, grad_pair, grad_slab)


def solution(mesh):
    in_specs = (
        P("ja", "ka", None),
        P("ja", "ka", None),
        P(),
        P(),
        P(),
        P(),
        P(),
        P(),
        P(),
        P("ka", "ja", None),
    )
    out_specs = (P("ka", "ja", None), P("ja", "ka", None), P("ja", "ka", None))
    return jax.shard_map(shards, mesh=mesh, in_specs=in_specs, out_specs=out_specs, check_vma=False)
```

```python
import jax
import jax.numpy as jnp
from jax import lax
from jax.experimental import pallas as pl
from jax.experimental.pallas import tpu as pltpu
from jax.sharding import PartitionSpec as P

f32, bf16 = jnp.float32, jnp.bfloat16
norm_eps = 1e-05

YH, Z, X, YL, CORE = 2, 8, 4, 2, 2
C = 2
NR = 8 // C
HR, QR = NR // 2, NR // 4
KR = (2, 2)
KG = (2, 2)
CI = 16 * NR
B = 96
T = (B, 128)
MIB = 2**20
MESH = pl.DeviceIdType.MESH
NT = (((1,), (1,)), ((), ()))
NN = (((1,), (0,)), ((), ()))
VM = pl.BlockSpec(memory_space=pltpu.VMEM)
HBM = pl.BlockSpec(memory_space=pl.ANY)


def split(values):
    hi = values.astype(bf16)
    return hi, (values - hi.astype(f32)).astype(bf16)


def dot(a, b, dims=NN):
    return lax.dot_general(a, b, dims, preferred_element_type=f32)


def dot3(a, b, dims=NN):
    a_hi, a_lo = split(a)
    b_hi, b_lo = split(b)
    both = dot(jnp.concatenate([a_hi, a_lo], 1), jnp.concatenate([b_hi, b_hi], dims[0][1][0]), dims)
    return both + dot(a_hi, b_lo, dims)


def mean(values):
    return jnp.mean(values, axis=-1, keepdims=True)


def normalise(values):
    center = values - mean(values)
    scale = lax.rsqrt(mean(center * center) + norm_eps)
    return center * scale, scale


def prepare(gain, gate, value, w_up, w_low, wc_hi, wc_lo):
    column = jnp.broadcast_to(gain[...], (128, 128)).T
    folded = jnp.concatenate([gate[...] * column, value[...] * column], 1)
    hi, lo = split(folded)
    w_up[:128] = hi
    w_up[128:] = hi
    w_low[...] = lo
    hi, lo = split(folded - jnp.mean(folded, axis=0, keepdims=True))
    wc_hi[...] = hi
    wc_lo[...] = lo


def gates(normed, w_up, w_low):
    hi, lo = split(normed)
    both = dot(jnp.concatenate([hi, lo], 1), w_up[...]) + dot(hi, w_low[...])
    return 1.0 / (1.0 + jnp.exp(-both[:, :128])), both[:, 128:]


def forward(values, w_up, w_low):
    s, v = gates(normalise(values)[0], w_up, w_low)
    return s * v


def pull(values, grad, w_up, w_low, wc_hi, wc_lo):
    normed, scale = normalise(values)
    s, v = gates(normed, w_up, w_low)
    d_value = grad * s
    d_gate = d_value * v * (1.0 - s)
    hi, lo = split(jnp.concatenate([d_gate, d_value], 1))
    d = dot(hi, wc_hi[...], NT) + dot(lo, wc_hi[...], NT) + dot(hi, wc_lo[...], NT)
    return scale * (d - normed * mean(d * normed))


def accumulate(dst, src):
    dims = src.shape[:-2]
    if not dims:
        dst[...] = dst[...] + src[...]
        return

    def step(i, _):
        accumulate(dst.at[i], src.at[i])
        return 0

    lax.fori_loop(0, dims[0], step, 0, unroll=True)


def repeat(n, body):
    def step(i, _):
        body(i)
        return 0

    lax.fori_loop(0, n, step, 0, unroll=True)


def run(n, body, events=()):
    def step(t, _):
        for at, event in events:
            pl.when(t == at)(event)
        body(t)
        return 0

    lax.fori_loop(0, n, step, 0)


def rows_in(src, dst, first, n):
    flat = dst.reshape(dst.shape[0] * dst.shape[1], 128)

    def body(u):
        row = first + u
        tile = jnp.concatenate([src[row], jnp.zeros((32, 128), f32)], 0).T
        flat[pl.ds(row, 128, stride=dst.shape[1]), :] = tile

    repeat(n, body)


def rows_out(src, dst, first, n):
    flat = src.reshape(src.shape[0] * src.shape[1], 128)

    def body(u):
        row = first + u
        dst[row] = flat[pl.ds(row, 128, stride=src.shape[1]), :].T[:B]

    repeat(n, body)


class Net:
    def __init__(self, ss, rs):
        self.ss, self.rs = ss, rs
        self.keys, self.sent = {}, []
        ja, ka = lax.axis_index("ja"), lax.axis_index("ka")
        self.yh, self.z = ja // 8, ja % 8
        self.x, self.yl, self.cc = ka // 4, (ka // 2) % 2, ka % 2
        self.yh1, self.yl1, self.cc1 = 1 - self.yh, 1 - self.yl, 1 - self.cc
        self.zs = {d: by_z((self.z + d + 8) % 8) for d in range(-4, 5)}
        z_at = {d: (self.z + d + 8) % 8 for d in (-1, 1)}
        self.xs = {d: by_x((self.x + d + 4) % 4) for d in range(-2, 3)}
        x_at = {d: (self.x + d + 4) % 4 for d in (-1, 1)}
        self.to = {
            "z+": (self.yh * 8 + z_at[1], ka),
            "z-": (self.yh * 8 + z_at[-1], ka),
            "yh": (self.yh1 * 8 + self.z, ka),
            "x+": (ja, x_at[1] * 4 + ka % 4),
            "x-": (ja, x_at[-1] * 4 + ka % 4),
            "yl": (ja, self.x * 4 + self.yl1 * 2 + self.cc),
            "cc": (ja, self.x * 4 + self.yl * 2 + self.cc1),
        }

    def greet(self):
        barrier = pltpu.get_barrier_semaphore()
        for dev in self.to.values():
            pl.semaphore_signal(barrier, inc=1, device_id=dev, device_id_type=MESH)
        return lambda: pl.semaphore_wait(barrier, len(self.to))

    def copy(self, src, dst, key, way):
        k = self.keys.setdefault(key, len(self.keys))
        return pltpu.make_async_remote_copy(
            src_ref=src(),
            dst_ref=dst(),
            send_sem=self.ss.at[k],
            recv_sem=self.rs.at[k],
            device_id=self.to[way],
            device_id_type=MESH,
        )

    def send(self, src, dst, key, way):
        self.copy(src, dst, key, way).start()
        self.sent.append((src, dst, key, way))

    def recv(self, dst, key, way):
        self.copy(dst, dst, key, way).wait_recv()

    def drain(self, *kinds):
        for entry in [e for e in self.sent if not kinds or e[2][:2] in kinds]:
            self.copy(*entry).wait_send()
            self.sent.remove(entry)


ways = ((0, 1, "+"), (1, -1, "-"))


def by_z(z):
    return z // 4, (z // 2) % 2, z % 2


def by_x(x):
    return x // 2, x % 2


def UP(rows):
    return (rows + 1) // 2


def halves(lo, hi):
    mid = (lo + hi) // 2
    return (lo, mid), (mid, hi)


U, V = (0, HR), (HR, NR)
streams = {"u": U, "v": V, "a": U}


def rows_of(stream, d, end):
    return halves(*streams[stream])[d] if end else streams[stream]


class GatherJa:
    def __init__(self, net, W, c):
        self.n, self.W, self.c = net, W, c

    def at(self, yh, z, lo, hi):
        return lambda: self.W.at[(self.c, yh) + z + (pl.ds(lo, hi - lo),)]

    def piece(self, stream, d, z, s):
        return self.at(self.n.yh1 if stream == "a" else self.n.yh, z, *rows_of(stream, d, s == 4))

    def hop(self, stream, s):
        for d, sign, w in ways:
            ref = self.piece(stream, d, self.n.zs[-sign * (s - 1)], s)
            self.n.send(ref, ref, ("ag", self.c, stream, d, s), "z" + w)

    def over(self, d, rows):
        ref = self.at(self.n.yh, self.n.zs[d], *rows)
        self.n.send(ref, ref, ("agy", self.c, d, rows), "yh")

    def over_got(self, d, rows):
        self.n.recv(self.at(self.n.yh1, self.n.zs[d], *rows), ("agy", self.c, d, rows), "yh")

    def start(self):
        self.hop("u", 1)
        self.over(0, U)
        self.hop("v", 1)
        self.over(0, V)

    def start_a(self):
        self.over_got(0, U)
        self.hop("a", 1)

    def step(self, stream, s):
        def event():
            for d, sign, w in ways:
                ref = self.piece(stream, d, self.n.zs[-sign * s], s)
                self.n.recv(ref, ("ag", self.c, stream, d, s), "z" + w)
            if s < 4:
                self.hop(stream, s + 1)
            if stream == "v":
                for d in (-s, s) if s < 4 else (4,):
                    self.over(d, V)

        return event

    def finish(self):
        for d in (0, -1, 1, -2, 2, -3, 3, 4):
            self.over_got(d, V)


class ScatterKa:
    def __init__(self, net, Pn, Q, bufs, c):
        self.n, self.Pn, self.Q, self.c = net, Pn, Q, c
        self.x1a, self.x1b, self.y2, self.x2a, self.x2b, self.y1 = bufs
        self.k = KR[c]
        self.first, self.second = (0, self.k), (self.k, NR)

    def q(self, x, yl, lo, hi):
        return lambda: self.Q.at[(self.c,) + x + (slice(None) if yl is None else yl, pl.ds(lo, hi - lo))]

    def land(self, buf, rows, *where):
        return lambda: buf.at[(self.c,) + where + (pl.ds(0, rows[1] - rows[0]),)]

    def start(self):
        n, c = self.n, self.c
        n.send(lambda: self.Pn.at[c, :, :, :, n.cc1], lambda: self.Q.at[c], ("core", c), "cc")

    def far(self, buf, key, rows, yl):
        for d, sign, w in ways:
            part = halves(*rows)[d]
            if part[0] < part[1]:
                where = (d, slice(None)) if yl is None else (d,)
                self.n.send(self.q(self.n.xs[2], yl, *part), self.land(buf, part, *where), (key, self.c, d), "x" + w)

    def near(self, far, far_key, buf, key, rows, yl):
        for d, sign, w in ways:
            part = halves(*rows)[d]
            where = (d, slice(None)) if yl is None else (d,)
            if part[0] < part[1]:
                land = self.land(far, part, *where)
                self.n.recv(land, (far_key, self.c, d), "x" + w)
                accumulate(self.q(self.n.xs[sign], yl, *part)(), land())
            self.n.send(self.q(self.n.xs[sign], yl, *rows), self.land(buf, rows, *where), (key, self.c, d), "x" + w)

    def last(self, buf, key, rows, yl):
        for d, sign, w in ways:
            land = self.land(buf, rows, *((d, slice(None)) if yl is None else (d,)))
            self.n.recv(land, (key, self.c, d), "x" + w)
            accumulate(self.q(self.n.xs[0], yl, *rows)(), land())

    def one(self):
        n, c = self.n, self.c
        n.recv(lambda: self.Q.at[c], ("core", c), "cc")
        accumulate(self.Q.at[c], self.Pn.at[c, :, :, :, n.cc])
        if self.k < NR:
            src = lambda: self.Q.at[c, :, :, n.yl1, pl.ds(self.k, NR - self.k)]
            n.send(src, self.land(self.y2, self.second, slice(None), slice(None)), ("y2", c), "yl")
        self.far(self.x1a, "x1a", self.first, None)

    def two(self):
        self.near(self.x1a, "x1a", self.x1b, "x1b", self.first, None)

    def three(self):
        n, c = self.n, self.c
        if self.k < NR:
            land = self.land(self.y2, self.second, slice(None), slice(None))
            n.recv(land, ("y2", c), "yl")
            accumulate(self.Q.at[c, :, :, n.yl, pl.ds(self.k, NR - self.k)], land())
            self.far(self.x2a, "x2a", self.second, n.yl)

    def four(self):
        n, c = self.n, self.c
        self.last(self.x1b, "x1b", self.first, None)
        n.send(self.q(n.xs[0], n.yl1, *self.first), self.land(self.y1, self.first), ("y1", c), "yl")

    def five(self):
        if self.k < NR:
            self.near(self.x2a, "x2a", self.x2b, "x2b", self.second, self.n.yl)

    def six(self):
        n, c = self.n, self.c
        n.recv(self.land(self.y1, self.first), ("y1", c), "yl")
        accumulate(self.q(n.xs[0], n.yl, *self.first)(), self.land(self.y1, self.first)())
        if self.k < NR:
            self.last(self.x2b, "x2b", self.second, n.yl)


class GatherKa:
    def __init__(self, net, G, c):
        self.n, self.G, self.c = net, G, c
        self.k = KG[c]
        self.first, self.second = (0, self.k), (self.k, NR)
        self.mixed = self.k < NR

    def g(self, x, yl, core, lo, hi):
        return lambda: self.G.at[(self.c,) + x + (yl, core, pl.ds(lo, hi - lo))]

    def put(self, key, way, x, yl, rows):
        if rows[0] < rows[1]:
            ref = self.g(x, yl, self.n.cc, *rows)
            self.n.send(ref, ref, ("gk", self.c) + key, way)

    def get(self, key, way, x, yl, rows, other=False):
        if rows[0] < rows[1]:
            self.n.recv(self.g(x, yl, self.n.cc1 if other else self.n.cc, *rows), ("gk", self.c) + key, way)

    def zero(self):
        n = self.n
        self.put(("y1",), "yl", n.xs[0], n.yl, self.first)
        for d, sign, w in ways:
            self.put(("x2", d), "x" + w, n.xs[0], n.yl, (0, NR))
        self.put(("c0",), "cc", n.xs[0], n.yl, (0, NR))
        self.put(("y2", 0), "yl", n.xs[0], n.yl, self.second)

    def one(self):
        n = self.n
        self.get(("y1",), "yl", n.xs[0], n.yl1, self.first)
        for d, sign, w in ways:
            self.put(("x1", d), "x" + w, n.xs[0], n.yl1, self.first)
        self.put(("c1",), "cc", n.xs[0], n.yl1, self.first)

    def two(self):
        n = self.n
        for d, sign, w in ways:
            src = n.xs[-sign]
            self.get(("x2", d), "x" + w, src, n.yl, (0, NR))
            self.put(("x2h", d), "x" + w, src, n.yl, halves(0, NR)[d])
            self.put(("y2", 1 + d), "yl", src, n.yl, self.second)
            self.put(("c2", d), "cc", src, n.yl, (0, NR))

    def three(self):
        n = self.n
        for d, sign, w in ways:
            src = n.xs[-sign]
            self.get(("x1", d), "x" + w, src, n.yl1, self.first)
            self.put(("x1h", d), "x" + w, src, n.yl1, halves(*self.first)[d])
            self.put(("c3", d), "cc", src, n.yl1, self.first)

    def four(self):
        n = self.n
        for d, sign, w in ways:
            self.get(("x2h", d), "x" + w, n.xs[2], n.yl, halves(0, NR)[d])
        self.put(("y2", 3), "yl", n.xs[2], n.yl, self.second)
        self.put(("c4",), "cc", n.xs[2], n.yl, (0, NR))

    def five(self):
        n = self.n
        for d, sign, w in ways:
            self.get(("x1h", d), "x" + w, n.xs[2], n.yl1, halves(*self.first)[d])
        self.put(("c5",), "cc", n.xs[2], n.yl1, self.first)

    def six(self):
        n = self.n
        for k, x in enumerate((n.xs[0], n.xs[-1], n.xs[1], n.xs[2])):
            self.get(("y2", k), "yl", x, n.yl1, self.second)
            self.put(("c6", k), "cc", x, n.yl1, self.second)

    def finish(self):
        n = self.n
        self.get(("c0",), "cc", n.xs[0], n.yl, (0, NR), True)
        self.get(("c1",), "cc", n.xs[0], n.yl1, self.first, True)
        for d, sign, w in ways:
            src = n.xs[-sign]
            self.get(("c2", d), "cc", src, n.yl, (0, NR), True)
            self.get(("c3", d), "cc", src, n.yl1, self.first, True)
        self.get(("c4",), "cc", n.xs[2], n.yl, (0, NR), True)
        self.get(("c5",), "cc", n.xs[2], n.yl1, self.first, True)
        for k, x in enumerate((n.xs[0], n.xs[-1], n.xs[1], n.xs[2])):
            self.get(("c6", k), "cc", x, n.yl1, self.second, True)


class ScatterJa:
    def __init__(self, net, N, bufs, c):
        self.n, self.N, self.c = net, N, c
        self.ry, self.first, self.rest, self.rf = bufs

    def block(self, stream, z, lo, hi):
        col = self.n.yh1 if stream == "a" else self.n.yh
        return lambda: self.N.at[(self.c, col) + z + (pl.ds(lo, hi - lo),)]

    def land(self, stream, d, s):
        k = "uva".index(stream)
        if s == 1:
            return lambda: self.first.at[self.c, k, d]
        return lambda: self.rest.at[self.c, k, d, s - 2]

    def push(self, stream, s):
        for d, sign, w in ways:
            src = self.block(stream, self.n.zs[sign * (5 - s)], *rows_of(stream, d, s == 1))
            self.n.send(src, self.land(stream, d, s), ("rs", self.c, stream, d, s), "z" + w)

    def over(self, d):
        n, c = self.n, self.c
        src = lambda: self.N.at[(c, n.yh1) + n.zs[d] + (pl.ds(HR, HR),)]
        n.send(src, lambda: self.ry.at[c, d + 3], ("rsy", c, d), "yh")

    def over_got(self, d):
        n, c = self.n, self.c
        n.recv(lambda: self.ry.at[c, d + 3], ("rsy", c, d), "yh")
        accumulate(self.block("v", n.zs[d], *V)(), self.ry.at[c, d + 3])

    def start(self):
        self.over(4)
        self.push("a", 1)
        self.push("u", 1)
        for d in (3, -3, 2, -2, 1, -1, 0):
            self.over(d)

    def start_v(self):
        self.over_got(4)
        self.push("v", 1)

    def step(self, stream, s):
        def event():
            for d, sign, w in ways:
                if stream == "v" and (s < 4 or d == 0):
                    self.over_got(sign * (4 - s))
                land = self.land(stream, d, s)
                self.n.recv(land, ("rs", self.c, stream, d, s), "z" + w)
                accumulate(self.block(stream, self.n.zs[sign * (4 - s)], *rows_of(stream, d, s == 1))(), land())
            if s < 4:
                self.push(stream, s + 1)
            elif stream == "a":
                src = self.block("a", self.n.zs[0], *U)
                self.n.send(src, lambda: self.rf.at[self.c], ("rsf", self.c), "yh")

        return event

    def finish(self):
        n, c = self.n, self.c
        n.recv(lambda: self.rf.at[c], ("rsf", c), "yh")
        accumulate(self.block("u", n.zs[0], *U)(), self.rf.at[c])


def events_of(net, W, Pn, Q, ka_bufs, G, N, ja_bufs):
    table = {}
    for c in range(C):
        ag, rk = GatherJa(net, W, c), ScatterKa(net, Pn, Q, ka_bufs, c)
        gk, rj = GatherKa(net, G, c), ScatterJa(net, N, ja_bufs, c)
        table[f"ag{c}.start"] = ag.start
        table[f"ag{c}.start_a"] = ag.start_a
        for s in range(1, 5):
            for stream in streams:
                table[f"ag{c}.{stream}{s}"] = ag.step(stream, s)
                table[f"rj{c}.{stream}{s}"] = rj.step(stream, s)
        table[f"ag{c}.finish"] = ag.finish
        for name in ("start", "one", "two", "three", "four", "five", "six"):
            table[f"rk{c}.{name}"] = getattr(rk, name)
        for name in ("zero", "one", "two", "three", "four", "five", "six", "finish"):
            table[f"gk{c}.{name}"] = getattr(gk, name)
        for name in ("start", "start_v", "finish"):
            table[f"rj{c}.{name}"] = getattr(rj, name)
    return table


ORDER = (
    "prepare_left", "left0", "entered", "ag0.start", "left1", "prepare_right", "loaded",
    ("right", (3, "ag0.u1"), (3, "ag0.start_a"), (5, "ag0.v1"), (8, "ag0.u2"), (11, "ag0.a1"), (13, "ag0.v2"), (16, "ag0.u3"), (19, "ag0.a2"), (21, "ag0.v3"), (23, "ag0.u4"), (23, "ag1.start")),
    "ag0.a3", "ag0.v4", "ag1.u1", "ag1.v1", "ag1.start_a", "ag0.a4", "ag1.u2", "ag0.finish",
    ("turn_left0", (1, "ag1.v2"), (7, "ag1.a1")), "sent_left0",
    ("product0", (4, "ag1.u3"), (9, "ag1.v3"), (13, "ag1.a2")),
    ("turn_product0", (1, "ag1.u4"), (3, "ag1.v4"), (6, "ag1.a3")), "rk0.start", "ag1.a4", "ag1.finish",
    ("turn_left1", (7, "rk0.one"), (7, "sent_product0")), "sent_left1", ("product1", (10, "rk0.two")),
    ("turn_product1", (1, "rk0.three"), (6, "rk0.four")), "rk1.start", "rk0.five", "rk1.one", "sent_product1",
    "rk0.six", "rows0", "gk0.zero", "rk1.two", "gk0.two", "rk1.three", "rk1.four", "gk0.one", "gk0.four", "rk1.five",
    "gk0.three", "rk1.six", "rows1", "gk1.zero", "gk0.five", "gk0.six", "gk0.finish",
    ("turn_grad0", (3, "gk1.one"), (5, "gk1.two")),
    ("left_product0", (5, "gk1.three"), (9, "gk1.four"), (13, "gk1.five")), ("turn_back0", (4, "gk1.six")),
    "rj0.start", "gk1.finish", ("turn_grad1", (7, "rj0.a1")),
    ("left_product1", (1, "rj0.start_v"), (1, "rj0.u1"), (8, "rj0.a2"), (12, "rj0.v1"), (14, "rj0.u2")),
    ("turn_back1", (3, "rj0.a3"), (7, "rj0.v2")), "rj1.start", "rj0.u3",
    ("right_product", (3, "rj0.a4"), (6, "rj1.start_v"), (6, "rj0.v3"), (8, "rj1.a1"), (9, "rj1.u1"), (11, "rj0.u4"), (14, "rj1.v1")),
    "rj0.v4",
    ("right_pull", (2, "rj1.a2"), (3, "rj1.u2"), (5, "rj1.v2"), (6, "rj1.a3"), (6, "save0"), (7, "rj0.finish"), (7, "left_pull0"), (7, "rj1.u3"), (8, "rj1.v3"), (10, "rj1.a4"), (11, "rj1.u4"), (12, "save1"), (13, "rj1.v4"), (14, "rj1.finish"), (18, "save2")),
    "save3", "left_pull1",
)


def kernel(
    pair, slab, gain, left_gate, left_value, right_gate, right_value, out_gain, out_weight, cot,
    update, grad_pair, grad_slab,
    xv, wl_up, wl_low, wlc_hi, wlc_lo, wr_up, wr_low, wrc_hi, wrc_lo,
    W, Rt, Lt, Gt, Hb, N, Q, x1a, x1b, y2, x2a, x2b, y1, ry, first, rest, rf, ss, rs, local,
):
    net = Net(ss, rs)
    entered = net.greet()
    load = pltpu.make_async_copy(pair, xv, local.at[0])
    load.start()
    G, Pn = W, N
    events = events_of(net, W, Pn, Q, (x1a, x1b, y2, x2a, x2b, y1), G, N, (ry, first, rest, rf))

    Wf = W.reshape(C * 16 * NR, B, 128)
    Nf = N.reshape(C * 16 * NR, B, 128)
    flat_R = Rt.reshape(128 * B, 128)
    flat_H = Hb.reshape(128 * 128, 128)
    K = 4

    def right(t):
        made = forward(xv[pl.ds(t * K, K)].reshape(K * B, 128), wr_up, wr_low)
        for u in range(K):
            tile = jnp.concatenate([made[u * B : (u + 1) * B], jnp.zeros((32, 128), f32)], 0).T
            flat_R[pl.ds(t * K + u, 128, stride=B), :] = tile

    def each_h(make):
        def body(t):
            repeat(8, lambda u: make(t * 8 + u))

        return body

    def product(c):
        def make(h):
            Hb[h, c * CI : (c + 1) * CI, :B] = dot3(Lt[h, c * CI : (c + 1) * CI, :], Rt[h], NT)

        return each_h(make)

    def left_product(c):
        def make(h):
            turned = jnp.concatenate([Rt[h], jnp.zeros((32, 128), f32)], 0)
            Hb[h, c * CI : (c + 1) * CI, :] = dot3(Gt[h, c * CI : (c + 1) * CI, :], turned)

        return each_h(make)

    def right_product(h):
        Hb[h, :B, :] = dot3(Gt[h].T, Lt[h])[:B]

    def right_pull(t):
        grads = [flat_H[pl.ds(t * K + u, 128, stride=128), :].T[:B] for u in range(K)]
        rows = xv[pl.ds(t * K, K)].reshape(K * B, 128)
        out = pull(rows, jnp.concatenate(grads, 0), wr_up, wr_low, wrc_hi, wrc_lo)
        xv[pl.ds(t * K, K)] = out.reshape(K, B, 128)

    loops = {
        "right": (B // K, right),
        "right_product": (16, each_h(right_product)),
        "right_pull": (B // K, right_pull),
    }

    def turn_in(dst, c):
        return lambda t: rows_in(Wf, dst, c * CI + t * 8, 8)

    def turn_out(c):
        return lambda t: rows_out(Hb, Nf, c * CI + t * 8, 8)

    for c in range(C):
        loops[f"turn_left{c}"] = (CI // 8, turn_in(Lt, c))
        loops[f"product{c}"] = (16, product(c))
        loops[f"turn_product{c}"] = (CI // 8, turn_out(c))
        loops[f"turn_grad{c}"] = (CI // 8, turn_in(Gt, c))
        loops[f"left_product{c}"] = (16, left_product(c))
        loops[f"turn_back{c}"] = (CI // 8, turn_out(c))

    def left(c):
        def step():
            own = forward(slab[c * NR : (c + 1) * NR].reshape(NR * B, 128), wl_up, wl_low)
            W[(c, net.yh) + net.zs[0]] = own.reshape(NR, B, 128)

        return step

    def rows(c):
        def step():
            mine = (c,) + net.xs[0] + (net.yl,)

            def one(u):
                r = c * NR + u
                normed, scale = normalise(Q[mine + (u,)])
                update[r] = dot3(normed * out_gain[...], out_weight[...])
                d = dot3(cot[r], out_weight[...], NT) * out_gain[...]
                G[mine + (net.cc, u)] = scale * (d - mean(d) - normed * mean(d * normed))

            repeat(NR, one)

        return step

    def left_pull(c):
        def step():
            grads = N[(c, net.yh) + net.zs[0]].reshape(NR * B, 128)
            out = pull(slab[c * NR : (c + 1) * NR].reshape(NR * B, 128), grads, wl_up, wl_low, wlc_hi, wlc_lo)
            grad_slab[c * NR : (c + 1) * NR] = out.reshape(NR, B, 128)

        return step

    def save(k):
        part = pl.ds(k * (B // 4), B // 4)
        return pltpu.make_async_copy(xv.at[part], grad_pair.at[part], local.at[1 + k])

    steps = {
        "prepare_left": lambda: prepare(gain, left_gate, left_value, wl_up, wl_low, wlc_hi, wlc_lo),
        "prepare_right": lambda: prepare(gain, right_gate, right_value, wr_up, wr_low, wrc_hi, wrc_lo),
        "entered": entered,
        "loaded": load.wait,
    }
    for k in range(4):
        steps[f"save{k}"] = lambda k=k: save(k).start()
    for c in range(C):
        steps[f"left{c}"] = left(c)
        steps[f"rows{c}"] = rows(c)
        steps[f"left_pull{c}"] = left_pull(c)
        steps[f"sent_left{c}"] = lambda c=c: net.drain(("ag", c), ("agy", c))
        steps[f"sent_product{c}"] = lambda c=c: net.drain(("core", c))
    steps.update(events)

    for entry in ORDER:
        if isinstance(entry, str):
            steps[entry]()
        else:
            run(*loops[entry[0]], [(t, steps[name]) for t, name in entry[1:]])
    net.drain()
    for k in range(4):
        save(k).wait()


def shards(
    pair_map, slab_rows, norm_gain, left_gate, left_value, right_gate, right_value, out_gain, out_weight, cotangent
):
    S = jax.ShapeDtypeStruct
    M = pltpu.VMEM
    weights = [M((256, 256), bf16)] + [M((128, 256), bf16)] * 3
    return pl.pallas_call(
        kernel,
        out_shape=[S((8,) + T, f32), S((B,) + T, f32), S((8,) + T, f32)],
        in_specs=[HBM] + [VM] * 9,
        out_specs=[VM, HBM, VM],
        scratch_shapes=[M((B,) + T, f32)]
        + weights * 2
        + [
            M((C, 2, 2, 2, 2, NR) + T, f32),
            M((128, B, 128), f32),
            M((128, 128, 128), f32),
            M((128, 128, 128), f32),
            M((128, 128, 128), f32),
            M((C, 2, 2, 2, 2, NR) + T, f32),
            M((C, 2, 2, 2, NR) + T, f32),
            M((C, 2, YL, UP(max(KR))) + T, f32),
            M((C, 2, YL, max(KR)) + T, f32),
            M((C, 2, 2, max(NR - min(KR), 1)) + T, f32),
            M((C, 2, max(UP(NR - min(KR)), 1)) + T, f32),
            M((C, 2, max(NR - min(KR), 1)) + T, f32),
            M((C, max(KR)) + T, f32),
            M((C, Z, HR) + T, f32),
            M((C, 3, 2, QR) + T, f32),
            M((C, 3, 2, 3, HR) + T, f32),
            M((C, HR) + T, f32),
            pltpu.SemaphoreType.DMA((240,)),
            pltpu.SemaphoreType.DMA((240,)),
            pltpu.SemaphoreType.DMA((5,)),
        ],
        compiler_params=pltpu.CompilerParams(collective_id=1, has_side_effects=True, vmem_limit_bytes=63 * MIB),
        name="triangle",
    )(
        pair_map, slab_rows, norm_gain.reshape(1, 128), left_gate, left_value, right_gate, right_value,
        out_gain.reshape(1, 128), out_weight, cotangent,
    )


def solution(mesh):
    in_specs = (
        P("ja", "ka", None),
        P("ja", "ka", None),
        P(),
        P(),
        P(),
        P(),
        P(),
        P(),
        P(),
        P("ka", "ja", None),
    )
    out_specs = (P("ka", "ja", None), P("ja", "ka", None), P("ja", "ka", None))
    return jax.shard_map(shards, mesh=mesh, in_specs=in_specs, out_specs=out_specs, check_vma=False)
```

```python
from types import SimpleNamespace

import jax
import jax.numpy as jnp
from jax import lax
from jax.experimental import pallas as pl
from jax.experimental.pallas import tpu as pltpu
from jax.sharding import PartitionSpec as P

f32, bf16 = jnp.float32, jnp.bfloat16
norm_eps = 1e-05

YH, Z, X, YL, CORE = 2, 8, 4, 2, 2
C = 2
NR = 8 // C
HR, QR = NR // 2, NR // 4
KR = (2, 2)
KG = (2, 2)
CI = 16 * NR
B = 96
HS = 136
T = (B, 128)
MIB = 2**20
MESH = pl.DeviceIdType.MESH
NT = (((1,), (1,)), ((), ()))
NN = (((1,), (0,)), ((), ()))
VM = pl.BlockSpec(memory_space=pltpu.VMEM)
HBM = pl.BlockSpec(memory_space=pl.ANY)


def split(values):
    hi = values.astype(bf16)
    return hi, (values - hi.astype(f32)).astype(bf16)


def dot(a, b, dims=NN):
    return lax.dot_general(a, b, dims, preferred_element_type=f32)


def dot3(a, b, dims=NN):
    a_hi, a_lo = split(a)
    b_hi, b_lo = split(b)
    both = dot(jnp.concatenate([a_hi, a_lo], 1), jnp.concatenate([b_hi, b_hi], dims[0][1][0]), dims)
    return both + dot(a_hi, b_lo, dims)


def dot3_wide(a, b):
    a_hi, a_lo = split(a)
    b_hi, b_lo = split(b)
    upper = jnp.concatenate([b_hi, b_lo], 1)
    lower = jnp.concatenate([b_hi, jnp.zeros_like(b_lo)], 1)
    both = dot(jnp.concatenate([a_hi, a_lo], 1), jnp.concatenate([upper, lower], 0))
    return both[:, : b.shape[1]] + both[:, b.shape[1] :]


def mean(values):
    return jnp.mean(values, axis=-1, keepdims=True)


def normalise(values):
    center = values - mean(values)
    scale = lax.rsqrt(mean(center * center) + norm_eps)
    return center * scale, scale


def prepare(gain, gate, value, w_up, w_low, wc_hi, wc_lo):
    column = jnp.broadcast_to(gain[...], (128, 128)).T
    folded = jnp.concatenate([gate[...] * column, value[...] * column], 1)
    hi, lo = split(folded)
    w_up[:128] = hi
    w_up[128:] = hi
    w_low[...] = lo
    hi, lo = split(folded - jnp.mean(folded, axis=0, keepdims=True))
    wc_hi[...] = hi
    wc_lo[...] = lo


def gates(normed, w_up, w_low):
    hi, lo = split(normed)
    both = dot(jnp.concatenate([hi, lo], 1), w_up[...]) + dot(hi, w_low[...])
    return 1.0 / (1.0 + jnp.exp(-both[:, :128])), both[:, 128:]


def forward(values, w_up, w_low):
    s, v = gates(normalise(values)[0], w_up, w_low)
    return s * v


def pull(values, grad, w_up, w_low, wc_hi, wc_lo):
    normed, scale = normalise(values)
    s, v = gates(normed, w_up, w_low)
    d_value = grad * s
    d_gate = d_value * v * (1.0 - s)
    hi, lo = split(jnp.concatenate([d_gate, d_value], 1))
    d = dot(hi, wc_hi[...], NT) + dot(lo, wc_hi[...], NT) + dot(hi, wc_lo[...], NT)
    return scale * (d - normed * mean(d * normed))


def accumulate(dst, src):
    dims = src.shape[:-2]
    if not dims:
        dst[...] = dst[...] + src[...]
        return

    def step(i, _):
        accumulate(dst.at[i], src.at[i])
        return 0

    lax.fori_loop(0, dims[0], step, 0, unroll=True)


def repeat(n, body):
    def step(i, _):
        body(i)
        return 0

    lax.fori_loop(0, n, step, 0, unroll=True)


def run(n, body, events=()):
    def step(t, _):
        for at, event in events:
            pl.when(t == at)(event)
        body(t)
        return 0

    lax.fori_loop(0, n, step, 0)


def rows_in(src, dst, first, n):
    flat = dst.reshape(dst.shape[0] * dst.shape[1], 128)

    def body(u):
        row = first + u
        tile = jnp.concatenate([src[row], jnp.zeros((32, 128), f32)], 0).T
        flat[pl.ds(row, 128, stride=dst.shape[1]), :] = tile

    repeat(n, body)


def rows_out(src, dst, first, n):
    flat = src.reshape(src.shape[0] * src.shape[1], 128)

    def body(u):
        row = first + u
        dst[row] = flat[pl.ds(row, 128, stride=src.shape[1]), :].T[:B]

    repeat(n, body)


class Net:
    def __init__(self, ss, rs):
        self.ss, self.rs = ss, rs
        self.keys, self.sent = {}, []
        ja, ka = lax.axis_index("ja"), lax.axis_index("ka")
        self.yh, self.z = ja // 8, ja % 8
        self.x, self.yl, self.cc = ka // 4, (ka // 2) % 2, ka % 2
        self.yh1, self.yl1, self.cc1 = 1 - self.yh, 1 - self.yl, 1 - self.cc
        self.zs = {d: by_z((self.z + d + 8) % 8) for d in range(-4, 5)}
        z_at = {d: (self.z + d + 8) % 8 for d in (-1, 1)}
        self.xs = {d: by_x((self.x + d + 4) % 4) for d in range(-2, 3)}
        x_at = {d: (self.x + d + 4) % 4 for d in (-1, 1)}
        self.to = {
            "z+": (self.yh * 8 + z_at[1], ka),
            "z-": (self.yh * 8 + z_at[-1], ka),
            "yh": (self.yh1 * 8 + self.z, ka),
            "x+": (ja, x_at[1] * 4 + ka % 4),
            "x-": (ja, x_at[-1] * 4 + ka % 4),
            "yl": (ja, self.x * 4 + self.yl1 * 2 + self.cc),
            "cc": (ja, self.x * 4 + self.yl * 2 + self.cc1),
        }

    def greet(self):
        barrier = pltpu.get_barrier_semaphore()
        for dev in self.to.values():
            pl.semaphore_signal(barrier, inc=1, device_id=dev, device_id_type=MESH)
        return lambda: pl.semaphore_wait(barrier, len(self.to))

    def copy(self, src, dst, key, way):
        k = self.keys.setdefault(key, len(self.keys))
        return pltpu.make_async_remote_copy(
            src_ref=src(),
            dst_ref=dst(),
            send_sem=self.ss.at[k],
            recv_sem=self.rs.at[k],
            device_id=self.to[way],
            device_id_type=MESH,
        )

    def send(self, src, dst, key, way):
        self.copy(src, dst, key, way).start()
        self.sent.append((src, dst, key, way))

    def recv(self, dst, key, way):
        self.copy(dst, dst, key, way).wait_recv()

    def drain(self, *kinds):
        for entry in [e for e in self.sent if not kinds or e[2][:2] in kinds]:
            self.copy(*entry).wait_send()
            self.sent.remove(entry)


ways = ((0, 1, "+"), (1, -1, "-"))


def by_z(z):
    return z // 4, (z // 2) % 2, z % 2


def by_x(x):
    return x // 2, x % 2


def UP(rows):
    return (rows + 1) // 2


def halves(lo, hi):
    mid = (lo + hi) // 2
    return (lo, mid), (mid, hi)


U, V = (0, HR), (HR, NR)
streams = {"u": U, "v": V, "a": U}


def rows_of(stream, d, end):
    return halves(*streams[stream])[d] if end else streams[stream]


class GatherJa:
    def __init__(self, net, W, c):
        self.n, self.W, self.c = net, W, c
        self.u, self.v, self.a = [{s: self.step(k, s) for s in range(1, 5)} for k in streams]

    def at(self, yh, z, lo, hi):
        return lambda: self.W.at[(self.c, yh) + z + (pl.ds(lo, hi - lo),)]

    def piece(self, stream, d, z, s):
        return self.at(self.n.yh1 if stream == "a" else self.n.yh, z, *rows_of(stream, d, s == 4))

    def hop(self, stream, s):
        for d, sign, w in ways:
            ref = self.piece(stream, d, self.n.zs[-sign * (s - 1)], s)
            self.n.send(ref, ref, ("ag", self.c, stream, d, s), "z" + w)

    def over(self, d, rows):
        ref = self.at(self.n.yh, self.n.zs[d], *rows)
        self.n.send(ref, ref, ("agy", self.c, d, rows), "yh")

    def over_got(self, d, rows):
        self.n.recv(self.at(self.n.yh1, self.n.zs[d], *rows), ("agy", self.c, d, rows), "yh")

    def start(self):
        self.hop("u", 1)
        self.over(0, U)
        self.hop("v", 1)
        self.over(0, V)

    def start_a(self):
        self.over_got(0, U)
        self.hop("a", 1)

    def step(self, stream, s):
        def event():
            for d, sign, w in ways:
                ref = self.piece(stream, d, self.n.zs[-sign * s], s)
                self.n.recv(ref, ("ag", self.c, stream, d, s), "z" + w)
            if s < 4:
                self.hop(stream, s + 1)
            if stream == "v":
                for d in (-s, s) if s < 4 else (4,):
                    self.over(d, V)

        return event

    def finish(self):
        for d in (0, -1, 1, -2, 2, -3, 3, 4):
            self.over_got(d, V)


class ScatterKa:
    def __init__(self, net, Pn, Q, bufs, c):
        self.n, self.Pn, self.Q, self.c = net, Pn, Q, c
        self.x1a, self.x1b, self.y2, self.x2a, self.x2b, self.y1 = bufs
        self.k = KR[c]
        self.first, self.second = (0, self.k), (self.k, NR)

    def q(self, x, yl, lo, hi):
        return lambda: self.Q.at[(self.c,) + x + (slice(None) if yl is None else yl, pl.ds(lo, hi - lo))]

    def land(self, buf, rows, *where):
        return lambda: buf.at[(self.c,) + where + (pl.ds(0, rows[1] - rows[0]),)]

    def start(self):
        n, c = self.n, self.c
        n.send(lambda: self.Pn.at[c, :, :, :, n.cc1], lambda: self.Q.at[c], ("core", c), "cc")

    def far(self, buf, key, rows, yl):
        for d, sign, w in ways:
            part = halves(*rows)[d]
            if part[0] < part[1]:
                where = (d, slice(None)) if yl is None else (d,)
                self.n.send(self.q(self.n.xs[2], yl, *part), self.land(buf, part, *where), (key, self.c, d), "x" + w)

    def near(self, far, far_key, buf, key, rows, yl):
        for d, sign, w in ways:
            part = halves(*rows)[d]
            where = (d, slice(None)) if yl is None else (d,)
            if part[0] < part[1]:
                land = self.land(far, part, *where)
                self.n.recv(land, (far_key, self.c, d), "x" + w)
                accumulate(self.q(self.n.xs[sign], yl, *part)(), land())
            self.n.send(self.q(self.n.xs[sign], yl, *rows), self.land(buf, rows, *where), (key, self.c, d), "x" + w)

    def last(self, buf, key, rows, yl):
        for d, sign, w in ways:
            land = self.land(buf, rows, *((d, slice(None)) if yl is None else (d,)))
            self.n.recv(land, (key, self.c, d), "x" + w)
            accumulate(self.q(self.n.xs[0], yl, *rows)(), land())

    def one(self):
        n, c = self.n, self.c
        n.recv(lambda: self.Q.at[c], ("core", c), "cc")
        accumulate(self.Q.at[c], self.Pn.at[c, :, :, :, n.cc])
        if self.k < NR:
            src = lambda: self.Q.at[c, :, :, n.yl1, pl.ds(self.k, NR - self.k)]
            n.send(src, self.land(self.y2, self.second, slice(None), slice(None)), ("y2", c), "yl")
        self.far(self.x1a, "x1a", self.first, None)

    def two(self):
        self.near(self.x1a, "x1a", self.x1b, "x1b", self.first, None)

    def three(self):
        n, c = self.n, self.c
        if self.k < NR:
            land = self.land(self.y2, self.second, slice(None), slice(None))
            n.recv(land, ("y2", c), "yl")
            accumulate(self.Q.at[c, :, :, n.yl, pl.ds(self.k, NR - self.k)], land())
            self.far(self.x2a, "x2a", self.second, n.yl)

    def four(self):
        n, c = self.n, self.c
        self.last(self.x1b, "x1b", self.first, None)
        n.send(self.q(n.xs[0], n.yl1, *self.first), self.land(self.y1, self.first), ("y1", c), "yl")

    def five(self):
        if self.k < NR:
            self.near(self.x2a, "x2a", self.x2b, "x2b", self.second, self.n.yl)

    def six(self):
        n, c = self.n, self.c
        n.recv(self.land(self.y1, self.first), ("y1", c), "yl")
        accumulate(self.q(n.xs[0], n.yl, *self.first)(), self.land(self.y1, self.first)())
        if self.k < NR:
            self.last(self.x2b, "x2b", self.second, n.yl)


class GatherKa:
    def __init__(self, net, G, c):
        self.n, self.G, self.c = net, G, c
        self.k = KG[c]
        self.first, self.second = (0, self.k), (self.k, NR)
        self.mixed = self.k < NR

    def g(self, x, yl, core, lo, hi):
        return lambda: self.G.at[(self.c,) + x + (yl, core, pl.ds(lo, hi - lo))]

    def put(self, key, way, x, yl, rows):
        if rows[0] < rows[1]:
            ref = self.g(x, yl, self.n.cc, *rows)
            self.n.send(ref, ref, ("gk", self.c) + key, way)

    def get(self, key, way, x, yl, rows, other=False):
        if rows[0] < rows[1]:
            self.n.recv(self.g(x, yl, self.n.cc1 if other else self.n.cc, *rows), ("gk", self.c) + key, way)

    def zero(self):
        n = self.n
        self.put(("y1",), "yl", n.xs[0], n.yl, self.first)
        for d, sign, w in ways:
            self.put(("x2", d), "x" + w, n.xs[0], n.yl, (0, NR))
        self.put(("c0",), "cc", n.xs[0], n.yl, (0, NR))
        self.put(("y2", 0), "yl", n.xs[0], n.yl, self.second)

    def one(self):
        n = self.n
        self.get(("y1",), "yl", n.xs[0], n.yl1, self.first)
        for d, sign, w in ways:
            self.put(("x1", d), "x" + w, n.xs[0], n.yl1, self.first)
        self.put(("c1",), "cc", n.xs[0], n.yl1, self.first)

    def two(self):
        n = self.n
        for d, sign, w in ways:
            src = n.xs[-sign]
            self.get(("x2", d), "x" + w, src, n.yl, (0, NR))
            self.put(("x2h", d), "x" + w, src, n.yl, halves(0, NR)[d])
            self.put(("y2", 1 + d), "yl", src, n.yl, self.second)
            self.put(("c2", d), "cc", src, n.yl, (0, NR))

    def three(self):
        n = self.n
        for d, sign, w in ways:
            src = n.xs[-sign]
            self.get(("x1", d), "x" + w, src, n.yl1, self.first)
            self.put(("x1h", d), "x" + w, src, n.yl1, halves(*self.first)[d])
            self.put(("c3", d), "cc", src, n.yl1, self.first)

    def four(self):
        n = self.n
        for d, sign, w in ways:
            self.get(("x2h", d), "x" + w, n.xs[2], n.yl, halves(0, NR)[d])
        self.put(("y2", 3), "yl", n.xs[2], n.yl, self.second)
        self.put(("c4",), "cc", n.xs[2], n.yl, (0, NR))

    def five(self):
        n = self.n
        for d, sign, w in ways:
            self.get(("x1h", d), "x" + w, n.xs[2], n.yl1, halves(*self.first)[d])
        self.put(("c5",), "cc", n.xs[2], n.yl1, self.first)

    def six(self):
        n = self.n
        for k, x in enumerate((n.xs[0], n.xs[-1], n.xs[1], n.xs[2])):
            self.get(("y2", k), "yl", x, n.yl1, self.second)
            self.put(("c6", k), "cc", x, n.yl1, self.second)

    def finish(self):
        n = self.n
        self.get(("c0",), "cc", n.xs[0], n.yl, (0, NR), True)
        self.get(("c1",), "cc", n.xs[0], n.yl1, self.first, True)
        for d, sign, w in ways:
            src = n.xs[-sign]
            self.get(("c2", d), "cc", src, n.yl, (0, NR), True)
            self.get(("c3", d), "cc", src, n.yl1, self.first, True)
        self.get(("c4",), "cc", n.xs[2], n.yl, (0, NR), True)
        self.get(("c5",), "cc", n.xs[2], n.yl1, self.first, True)
        for k, x in enumerate((n.xs[0], n.xs[-1], n.xs[1], n.xs[2])):
            self.get(("c6", k), "cc", x, n.yl1, self.second, True)


class ScatterJa:
    def __init__(self, net, N, bufs, c):
        self.n, self.N, self.c = net, N, c
        self.ry, self.first, self.rest, self.rf = bufs
        self.u, self.v, self.a = [{s: self.step(k, s) for s in range(1, 5)} for k in streams]

    def block(self, stream, z, lo, hi):
        col = self.n.yh1 if stream == "a" else self.n.yh
        return lambda: self.N.at[(self.c, col) + z + (pl.ds(lo, hi - lo),)]

    def land(self, stream, d, s):
        k = "uva".index(stream)
        if s == 1:
            return lambda: self.first.at[self.c, k, d]
        return lambda: self.rest.at[self.c, k, d, s - 2]

    def push(self, stream, s):
        for d, sign, w in ways:
            src = self.block(stream, self.n.zs[sign * (5 - s)], *rows_of(stream, d, s == 1))
            self.n.send(src, self.land(stream, d, s), ("rs", self.c, stream, d, s), "z" + w)

    def over(self, d):
        n, c = self.n, self.c
        src = lambda: self.N.at[(c, n.yh1) + n.zs[d] + (pl.ds(HR, HR),)]
        n.send(src, lambda: self.ry.at[c, d + 3], ("rsy", c, d), "yh")

    def over_got(self, d):
        n, c = self.n, self.c
        n.recv(lambda: self.ry.at[c, d + 3], ("rsy", c, d), "yh")
        accumulate(self.block("v", n.zs[d], *V)(), self.ry.at[c, d + 3])

    def start(self):
        self.over(4)
        self.push("a", 1)
        self.push("u", 1)
        for d in (3, -3, 2, -2, 1, -1, 0):
            self.over(d)

    def start_v(self):
        self.over_got(4)
        self.push("v", 1)

    def step(self, stream, s):
        def event():
            for d, sign, w in ways:
                if stream == "v" and (s < 4 or d == 0):
                    self.over_got(sign * (4 - s))
                land = self.land(stream, d, s)
                self.n.recv(land, ("rs", self.c, stream, d, s), "z" + w)
                accumulate(self.block(stream, self.n.zs[sign * (4 - s)], *rows_of(stream, d, s == 1))(), land())
            if s < 4:
                self.push(stream, s + 1)
            elif stream == "a":
                src = self.block("a", self.n.zs[0], *U)
                self.n.send(src, lambda: self.rf.at[self.c], ("rsf", self.c), "yh")

        return event

    def finish(self):
        n, c = self.n, self.c
        n.recv(lambda: self.rf.at[c], ("rsf", c), "yh")
        accumulate(self.block("u", n.zs[0], *U)(), self.rf.at[c])


def order(ag, rk, gk, rj, do, loop):
    return (
        do.prepare_left, do.left[0], do.entered, ag[0].start, do.left[1], do.prepare_right, do.loaded, (loop.right,
        (2, ag[0].u[1]), (2, ag[0].start_a), (4, ag[0].v[1]), (5, ag[0].u[2]), (7, ag[0].a[1]), (9, ag[0].v[2]),
        (11, ag[0].u[3])), ag[0].a[2], ag[0].v[3], ag[0].u[4], ag[1].start, ag[0].a[3], ag[0].v[4], ag[1].u[1],
        ag[1].v[1], ag[1].start_a, ag[0].a[4], ag[1].u[2], ag[0].finish, (loop.turn_left[0], (1, ag[1].v[2]), (6,
        ag[1].a[1])), do.sent_left[0], (loop.product[0], (2, ag[1].u[3]), (4, ag[1].v[3]), (5, ag[1].a[2]), (7,
        ag[1].u[4])), ag[1].v[4], (loop.turn_product[0], (4, ag[1].a[3])), rk[0].start, ag[1].a[4], ag[1].finish,
        (loop.turn_left[1], (7, rk[0].one), (7, do.sent_product[0])), do.sent_left[1], (loop.product[1], (4,
        rk[0].two)), rk[0].three, (loop.turn_product[1], (3, rk[0].four)), rk[1].start, rk[0].five, rk[1].one,
        do.sent_product[1], rk[0].six, do.rows[0], gk[0].zero, rk[1].two, gk[0].two, rk[1].three, rk[1].four,
        gk[0].one, gk[0].four, rk[1].five, gk[0].three, rk[1].six, do.rows[1], gk[1].zero, gk[0].five, gk[0].six,
        gk[0].finish, (loop.turn_grad[0], (3, gk[1].one), (4, gk[1].two)), (loop.left_product[0], (3, gk[1].three),
        (5, gk[1].four)), gk[1].five, (loop.turn_back[0], (7, gk[1].six)), rj[0].start, gk[1].finish,
        (loop.turn_grad[1], (6, rj[0].a[1]), (7, rj[0].start_v), (7, rj[0].u[1])), (loop.left_product[1], (4,
        rj[0].a[2]), (6, rj[0].v[1])), rj[0].u[2], (loop.turn_back[1], (5, rj[0].a[3])), rj[1].start, rj[0].v[2],
        (loop.right_product, (2, rj[0].u[3]), (6, rj[0].a[4]), (9, rj[1].a[1]), (9, rj[1].start_v), (10,
        rj[1].u[1]), (12, rj[0].v[3])), rj[0].u[4], (loop.right_pull, (1, rj[1].a[2]), (2, rj[1].v[1]), (3,
        rj[1].u[2]), (3, do.save[0]), (4, rj[0].v[4]), (5, rj[1].a[3]), (6, rj[1].v[2]), (6, rj[0].finish), (6,
        do.left_pull[0]), (6, rj[1].u[3]), (6, do.save[1]), (7, rj[1].a[4]), (8, rj[1].v[3]), (9, rj[1].u[4]), (9,
        do.save[2]), (11, rj[1].v[4]), (11, rj[1].finish)), do.save[3], do.left_pull[1],
    )


def kernel(
    pair, slab, gain, left_gate, left_value, right_gate, right_value, out_gain, out_weight, cot,
    update, grad_pair, grad_slab,
    xv, wl_up, wl_low, wlc_hi, wlc_lo, wr_up, wr_low, wrc_hi, wrc_lo,
    W, Rt, Lt, Gt, Hb, N, Q, x1a, x1b, y2, x2a, x2b, y1, ry, first, rest, rf, ss, rs, local,
):
    net = Net(ss, rs)
    entered = net.greet()
    load = pltpu.make_async_copy(pair, xv, local.at[0])
    load.start()
    G, Pn = W, N
    each = range(C)
    ag = [GatherJa(net, W, c) for c in each]
    rk = [ScatterKa(net, Pn, Q, (x1a, x1b, y2, x2a, x2b, y1), c) for c in each]
    gk = [GatherKa(net, G, c) for c in each]
    rj = [ScatterJa(net, N, (ry, first, rest, rf), c) for c in each]

    Wf = W.reshape(C * 16 * NR, B, 128)
    Nf = N.reshape(C * 16 * NR, B, 128)
    flat_R = Rt.reshape(128 * B, 128)
    flat_H = Hb.reshape(128 * HS, 128)
    K = 8

    def right(t):
        made = forward(xv[pl.ds(t * K, K)].reshape(K * B, 128), wr_up, wr_low)
        for u in range(K):
            tile = jnp.concatenate([made[u * B : (u + 1) * B], jnp.zeros((32, 128), f32)], 0).T
            flat_R[pl.ds(t * K + u, 128, stride=B), :] = tile

    def each_h(n, make):
        return 128 // n, lambda t: repeat(n, lambda u: make(t * n + u))

    def product(c):
        def make(h):
            Hb[h, c * CI : (c + 1) * CI, :B] = dot3(Lt[h, c * CI : (c + 1) * CI, :], Rt[h], NT)

        return each_h(16, make)

    def left_product(c):
        def make(h):
            turned = jnp.concatenate([Rt[h], jnp.zeros((32, 128), f32)], 0)
            Hb[h, c * CI : (c + 1) * CI, :] = dot3_wide(Gt[h, c * CI : (c + 1) * CI, :], turned)

        return each_h(16, make)

    def right_product(h):
        Hb[h, :B, :] = dot3_wide(Gt[h].T, Lt[h])[:B]

    def right_pull(t):
        grads = [flat_H[pl.ds(t * K + u, 128, stride=HS), :].T[:B] for u in range(K)]
        rows = xv[pl.ds(t * K, K)].reshape(K * B, 128)
        out = pull(rows, jnp.concatenate(grads, 0), wr_up, wr_low, wrc_hi, wrc_lo)
        xv[pl.ds(t * K, K)] = out.reshape(K, B, 128)

    def turn_in(dst, c):
        return CI // 8, lambda t: rows_in(Wf, dst, c * CI + t * 8, 8)

    def turn_out(c):
        return CI // 8, lambda t: rows_out(Hb, Nf, c * CI + t * 8, 8)

    loop = SimpleNamespace(
        right=(B // K, right),
        turn_left=[turn_in(Lt, c) for c in each],
        product=[product(c) for c in each],
        turn_product=[turn_out(c) for c in each],
        turn_grad=[turn_in(Gt, c) for c in each],
        left_product=[left_product(c) for c in each],
        turn_back=[turn_out(c) for c in each],
        right_product=each_h(8, right_product),
        right_pull=(B // K, right_pull),
    )

    def left(c):
        def step():
            own = forward(slab[c * NR : (c + 1) * NR].reshape(NR * B, 128), wl_up, wl_low)
            W[(c, net.yh) + net.zs[0]] = own.reshape(NR, B, 128)

        return step

    def rows(c):
        def step():
            mine = (c,) + net.xs[0] + (net.yl,)

            def one(u):
                r = c * NR + u
                normed, scale = normalise(Q[mine + (u,)])
                update[r] = dot3(normed * out_gain[...], out_weight[...])
                d = dot3(cot[r], out_weight[...], NT) * out_gain[...]
                G[mine + (net.cc, u)] = scale * (d - mean(d) - normed * mean(d * normed))

            repeat(NR, one)

        return step

    def left_pull(c):
        def step():
            grads = N[(c, net.yh) + net.zs[0]].reshape(NR * B, 128)
            out = pull(slab[c * NR : (c + 1) * NR].reshape(NR * B, 128), grads, wl_up, wl_low, wlc_hi, wlc_lo)
            grad_slab[c * NR : (c + 1) * NR] = out.reshape(NR, B, 128)

        return step

    def save(k):
        part = pl.ds(k * (B // 4), B // 4)
        return pltpu.make_async_copy(xv.at[part], grad_pair.at[part], local.at[1 + k])

    do = SimpleNamespace(
        prepare_left=lambda: prepare(gain, left_gate, left_value, wl_up, wl_low, wlc_hi, wlc_lo),
        prepare_right=lambda: prepare(gain, right_gate, right_value, wr_up, wr_low, wrc_hi, wrc_lo),
        entered=entered,
        loaded=load.wait,
        left=[left(c) for c in each],
        rows=[rows(c) for c in each],
        left_pull=[left_pull(c) for c in each],
        save=[lambda k=k: save(k).start() for k in range(4)],
        sent_left=[lambda c=c: net.drain(("ag", c), ("agy", c)) for c in each],
        sent_product=[lambda c=c: net.drain(("core", c)) for c in each],
    )

    for entry in order(ag, rk, gk, rj, do, loop):
        if isinstance(entry, tuple):
            (n, body), *events = entry
            run(n, body, events)
        else:
            entry()
    net.drain()
    for k in range(4):
        save(k).wait()


def shards(
    pair_map, slab_rows, norm_gain, left_gate, left_value, right_gate, right_value, out_gain, out_weight, cotangent
):
    S = jax.ShapeDtypeStruct
    M = pltpu.VMEM
    weights = [M((256, 256), bf16)] + [M((128, 256), bf16)] * 3
    return pl.pallas_call(
        kernel,
        out_shape=[S((8,) + T, f32), S((B,) + T, f32), S((8,) + T, f32)],
        in_specs=[HBM] + [VM] * 9,
        out_specs=[VM, HBM, VM],
        scratch_shapes=[M((B,) + T, f32)]
        + weights * 2
        + [
            M((C, 2, 2, 2, 2, NR) + T, f32),
            M((128, B, 128), f32),
            M((128, 128, 128), f32),
            M((128, 128, 128), f32),
            M((128, HS, 128), f32),
            M((C, 2, 2, 2, 2, NR) + T, f32),
            M((C, 2, 2, 2, NR) + T, f32),
            M((C, 2, YL, UP(max(KR))) + T, f32),
            M((C, 2, YL, max(KR)) + T, f32),
            M((C, 2, 2, max(NR - min(KR), 1)) + T, f32),
            M((C, 2, max(UP(NR - min(KR)), 1)) + T, f32),
            M((C, 2, max(NR - min(KR), 1)) + T, f32),
            M((C, max(KR)) + T, f32),
            M((C, Z, HR) + T, f32),
            M((C, 3, 2, QR) + T, f32),
            M((C, 3, 2, 3, HR) + T, f32),
            M((C, HR) + T, f32),
            pltpu.SemaphoreType.DMA((240,)),
            pltpu.SemaphoreType.DMA((240,)),
            pltpu.SemaphoreType.DMA((5,)),
        ],
        compiler_params=pltpu.CompilerParams(collective_id=1, has_side_effects=True, vmem_limit_bytes=63 * MIB),
        name="triangle",
    )(
        pair_map, slab_rows, norm_gain.reshape(1, 128), left_gate, left_value, right_gate, right_value,
        out_gain.reshape(1, 128), out_weight, cotangent,
    )


def solution(mesh):
    in_specs = (
        P("ja", "ka", None),
        P("ja", "ka", None),
        P(),
        P(),
        P(),
        P(),
        P(),
        P(),
        P(),
        P("ka", "ja", None),
    )
    out_specs = (P("ka", "ja", None), P("ja", "ka", None), P("ja", "ka", None))
    return jax.shard_map(shards, mesh=mesh, in_specs=in_specs, out_specs=out_specs, check_vma=False)
```

```python
from types import SimpleNamespace

import jax
import jax.numpy as jnp
from jax import lax
from jax.experimental import pallas as pl
from jax.experimental.pallas import tpu as pltpu
from jax.sharding import PartitionSpec as P

f32, bf16 = jnp.float32, jnp.bfloat16
norm_eps = 1e-05

YH, Z, X, YL, CORE = 2, 8, 4, 2, 2
C = 2
NR = 8 // C
HR, QR = NR // 2, NR // 4
KR = (2, 2)
KG = (2, 2)
CI = 16 * NR
B = 96
HS = 136
T = (B, 128)
MIB = 2**20
MESH = pl.DeviceIdType.MESH
NT = (((1,), (1,)), ((), ()))
NN = (((1,), (0,)), ((), ()))
VM = pl.BlockSpec(memory_space=pltpu.VMEM)
HBM = pl.BlockSpec(memory_space=pl.ANY)


def split(values):
    hi = values.astype(bf16)
    return hi, (values - hi.astype(f32)).astype(bf16)


def dot(a, b, dims=NN):
    return lax.dot_general(a, b, dims, preferred_element_type=f32)


def dot3(a, b, dims=NN):
    a_hi, a_lo = split(a)
    b_hi, b_lo = split(b)
    both = dot(jnp.concatenate([a_hi, a_lo], 1), jnp.concatenate([b_hi, b_hi], dims[0][1][0]), dims)
    return both + dot(a_hi, b_lo, dims)


def dot3_wide(a, b):
    a_hi, a_lo = split(a)
    b_hi, b_lo = split(b)
    upper = jnp.concatenate([b_hi, b_lo], 1)
    lower = jnp.concatenate([b_hi, jnp.zeros_like(b_lo)], 1)
    both = dot(jnp.concatenate([a_hi, a_lo], 1), jnp.concatenate([upper, lower], 0))
    return both[:, : b.shape[1]] + both[:, b.shape[1] :]


def mean(values):
    return jnp.mean(values, axis=-1, keepdims=True)


def normalise(values):
    center = values - mean(values)
    scale = lax.rsqrt(mean(center * center) + norm_eps)
    return center * scale, scale


def prepare(gain, gate, value, w_up, w_low, wc_hi, wc_lo):
    column = jnp.broadcast_to(gain[...], (128, 128)).T
    folded = jnp.concatenate([gate[...] * column, value[...] * column], 1)
    hi, lo = split(folded)
    w_up[:128] = hi
    w_up[128:] = hi
    w_low[...] = lo
    hi, lo = split(folded - jnp.mean(folded, axis=0, keepdims=True))
    wc_hi[...] = hi
    wc_lo[...] = lo


def gates(normed, w_up, w_low):
    hi, lo = split(normed)
    both = dot(jnp.concatenate([hi, lo], 1), w_up[...]) + dot(hi, w_low[...])
    return 1.0 / (1.0 + jnp.exp(-both[:, :128])), both[:, 128:]


def forward(values, w_up, w_low):
    s, v = gates(normalise(values)[0], w_up, w_low)
    return s * v


def pull(values, grad, s, v, wc_hi, wc_lo):
    normed, scale = normalise(values)
    d_value = grad * s
    d_gate = d_value * v * (1.0 - s)
    hi, lo = split(jnp.concatenate([d_gate, d_value], 1))
    d = dot(hi, wc_hi[...], NT) + dot(lo, wc_hi[...], NT) + dot(hi, wc_lo[...], NT)
    return scale * (d - normed * mean(d * normed))


def accumulate(dst, src):
    dims = src.shape[:-2]
    if not dims:
        dst[...] = dst[...] + src[...]
        return

    def step(i, _):
        accumulate(dst.at[i], src.at[i])
        return 0

    lax.fori_loop(0, dims[0], step, 0, unroll=True)


def repeat(n, body):
    def step(i, _):
        body(i)
        return 0

    lax.fori_loop(0, n, step, 0, unroll=True)


def run(n, body, events=()):
    def step(t, _):
        for at, event in events:
            pl.when(t == at)(event)
        body(t)
        return 0

    lax.fori_loop(0, n, step, 0)


def rows_in(src, dst, first, n):
    flat = dst.reshape(dst.shape[0] * dst.shape[1], 128)

    def body(u):
        row = first + u
        tile = jnp.concatenate([src[row], jnp.zeros((32, 128), f32)], 0).T
        flat[pl.ds(row, 128, stride=dst.shape[1]), :] = tile

    repeat(n, body)


def rows_out(src, dst, first, n):
    flat = src.reshape(src.shape[0] * src.shape[1], 128)

    def body(u):
        row = first + u
        dst[row] = flat[pl.ds(row, 128, stride=src.shape[1]), :].T[:B]

    repeat(n, body)


class Net:
    def __init__(self, ss, rs):
        self.ss, self.rs = ss, rs
        self.keys, self.sent = {}, []
        ja, ka = lax.axis_index("ja"), lax.axis_index("ka")
        self.yh, self.z = ja // 8, ja % 8
        self.x, self.yl, self.cc = ka // 4, (ka // 2) % 2, ka % 2
        self.yh1, self.yl1, self.cc1 = 1 - self.yh, 1 - self.yl, 1 - self.cc
        self.zs = {d: by_z((self.z + d + 8) % 8) for d in range(-4, 5)}
        z_at = {d: (self.z + d + 8) % 8 for d in (-1, 1)}
        self.xs = {d: by_x((self.x + d + 4) % 4) for d in range(-2, 3)}
        x_at = {d: (self.x + d + 4) % 4 for d in (-1, 1)}
        self.to = {
            "z+": (self.yh * 8 + z_at[1], ka),
            "z-": (self.yh * 8 + z_at[-1], ka),
            "yh": (self.yh1 * 8 + self.z, ka),
            "x+": (ja, x_at[1] * 4 + ka % 4),
            "x-": (ja, x_at[-1] * 4 + ka % 4),
            "yl": (ja, self.x * 4 + self.yl1 * 2 + self.cc),
            "cc": (ja, self.x * 4 + self.yl * 2 + self.cc1),
        }

    def greet(self):
        barrier = pltpu.get_barrier_semaphore()
        for dev in self.to.values():
            pl.semaphore_signal(barrier, inc=1, device_id=dev, device_id_type=MESH)
        return lambda: pl.semaphore_wait(barrier, len(self.to))

    def copy(self, src, dst, key, way):
        k = self.keys.setdefault(key, len(self.keys))
        return pltpu.make_async_remote_copy(
            src_ref=src(),
            dst_ref=dst(),
            send_sem=self.ss.at[k],
            recv_sem=self.rs.at[k],
            device_id=self.to[way],
            device_id_type=MESH,
        )

    def send(self, src, dst, key, way):
        self.copy(src, dst, key, way).start()
        self.sent.append((src, dst, key, way))

    def recv(self, dst, key, way):
        self.copy(dst, dst, key, way).wait_recv()

    def drain(self, *kinds):
        for entry in [e for e in self.sent if not kinds or e[2][:2] in kinds]:
            self.copy(*entry).wait_send()
            self.sent.remove(entry)


ways = ((0, 1, "+"), (1, -1, "-"))


def by_z(z):
    return z // 4, (z // 2) % 2, z % 2


def by_x(x):
    return x // 2, x % 2


def UP(rows):
    return (rows + 1) // 2


def halves(lo, hi):
    mid = (lo + hi) // 2
    return (lo, mid), (mid, hi)


U, V = (0, HR), (HR, NR)
streams = {"u": U, "v": V, "a": U}


def rows_of(stream, d, end):
    return halves(*streams[stream])[d] if end else streams[stream]


class GatherJa:
    def __init__(self, net, W, c):
        self.n, self.W, self.c = net, W, c
        self.u, self.v, self.a = [{s: self.step(k, s) for s in range(1, 5)} for k in streams]

    def at(self, yh, z, lo, hi):
        return lambda: self.W.at[(self.c, yh) + z + (pl.ds(lo, hi - lo),)]

    def piece(self, stream, d, z, s):
        return self.at(self.n.yh1 if stream == "a" else self.n.yh, z, *rows_of(stream, d, s == 4))

    def hop(self, stream, s):
        for d, sign, w in ways:
            ref = self.piece(stream, d, self.n.zs[-sign * (s - 1)], s)
            self.n.send(ref, ref, ("ag", self.c, stream, d, s), "z" + w)

    def over(self, d, rows):
        ref = self.at(self.n.yh, self.n.zs[d], *rows)
        self.n.send(ref, ref, ("agy", self.c, d, rows), "yh")

    def over_got(self, d, rows):
        self.n.recv(self.at(self.n.yh1, self.n.zs[d], *rows), ("agy", self.c, d, rows), "yh")

    def start(self):
        self.hop("u", 1)
        self.over(0, U)
        self.hop("v", 1)
        self.over(0, V)

    def start_a(self):
        self.over_got(0, U)
        self.hop("a", 1)

    def step(self, stream, s):
        def event():
            for d, sign, w in ways:
                ref = self.piece(stream, d, self.n.zs[-sign * s], s)
                self.n.recv(ref, ("ag", self.c, stream, d, s), "z" + w)
            if s < 4:
                self.hop(stream, s + 1)
            if stream == "v":
                for d in (-s, s) if s < 4 else (4,):
                    self.over(d, V)

        return event

    def finish(self):
        for d in (0, -1, 1, -2, 2, -3, 3, 4):
            self.over_got(d, V)


class ScatterKa:
    def __init__(self, net, Pn, Q, bufs, c):
        self.n, self.Pn, self.Q, self.c = net, Pn, Q, c
        self.x1a, self.x1b, self.y2, self.x2a, self.x2b, self.y1 = bufs
        self.k = KR[c]
        self.first, self.second = (0, self.k), (self.k, NR)

    def q(self, x, yl, lo, hi):
        return lambda: self.Q.at[(self.c,) + x + (slice(None) if yl is None else yl, pl.ds(lo, hi - lo))]

    def land(self, buf, rows, *where):
        return lambda: buf.at[(self.c,) + where + (pl.ds(0, rows[1] - rows[0]),)]

    def halves_of_core(self):
        return [rows for rows in (self.second, self.first) if rows[0] < rows[1]]

    def start(self):
        n, c = self.n, self.c
        for k, (lo, hi) in enumerate(self.halves_of_core()):
            part = pl.ds(lo, hi - lo)
            src = lambda part=part: self.Pn.at[c, :, :, :, n.cc1, part]
            n.send(src, lambda part=part: self.Q.at[c, :, :, :, part], ("core", c, k), "cc")

    def far(self, buf, key, rows, yl):
        for d, sign, w in ways:
            part = halves(*rows)[d]
            if part[0] < part[1]:
                where = (d, slice(None)) if yl is None else (d,)
                self.n.send(self.q(self.n.xs[2], yl, *part), self.land(buf, part, *where), (key, self.c, d), "x" + w)

    def near(self, far, far_key, buf, key, rows, yl):
        for d, sign, w in ways:
            part = halves(*rows)[d]
            where = (d, slice(None)) if yl is None else (d,)
            if part[0] < part[1]:
                land = self.land(far, part, *where)
                self.n.recv(land, (far_key, self.c, d), "x" + w)
                accumulate(self.q(self.n.xs[sign], yl, *part)(), land())
            self.n.send(self.q(self.n.xs[sign], yl, *rows), self.land(buf, rows, *where), (key, self.c, d), "x" + w)

    def last(self, buf, key, rows, yl):
        for d, sign, w in ways:
            land = self.land(buf, rows, *((d, slice(None)) if yl is None else (d,)))
            self.n.recv(land, (key, self.c, d), "x" + w)
            accumulate(self.q(self.n.xs[0], yl, *rows)(), land())

    def one(self):
        n, c = self.n, self.c
        for k, (lo, hi) in enumerate(self.halves_of_core()):
            part = pl.ds(lo, hi - lo)
            n.recv(lambda: self.Q.at[c, :, :, :, part], ("core", c, k), "cc")
            accumulate(self.Q.at[c, :, :, :, part], self.Pn.at[c, :, :, :, n.cc, part])
            if lo > 0:
                land = self.land(self.y2, self.second, slice(None), slice(None))
                n.send(lambda part=part: self.Q.at[c, :, :, n.yl1, part], land, ("y2", c), "yl")
        self.far(self.x1a, "x1a", self.first, None)

    def two(self):
        self.near(self.x1a, "x1a", self.x1b, "x1b", self.first, None)

    def three(self):
        n, c = self.n, self.c
        if self.k < NR:
            land = self.land(self.y2, self.second, slice(None), slice(None))
            n.recv(land, ("y2", c), "yl")
            accumulate(self.Q.at[c, :, :, n.yl, pl.ds(self.k, NR - self.k)], land())
            self.far(self.x2a, "x2a", self.second, n.yl)

    def four(self):
        n, c = self.n, self.c
        self.last(self.x1b, "x1b", self.first, None)
        n.send(self.q(n.xs[0], n.yl1, *self.first), self.land(self.y1, self.first), ("y1", c), "yl")

    def five(self):
        if self.k < NR:
            self.near(self.x2a, "x2a", self.x2b, "x2b", self.second, self.n.yl)

    def six(self):
        n, c = self.n, self.c
        n.recv(self.land(self.y1, self.first), ("y1", c), "yl")
        accumulate(self.q(n.xs[0], n.yl, *self.first)(), self.land(self.y1, self.first)())
        if self.k < NR:
            self.last(self.x2b, "x2b", self.second, n.yl)


class GatherKa:
    def __init__(self, net, G, c):
        self.n, self.G, self.c = net, G, c
        self.k = KG[c]
        self.first, self.second = (0, self.k), (self.k, NR)
        self.mixed = self.k < NR

    def g(self, x, yl, core, lo, hi):
        return lambda: self.G.at[(self.c,) + x + (yl, core, pl.ds(lo, hi - lo))]

    def put(self, key, way, x, yl, rows):
        if rows[0] < rows[1]:
            ref = self.g(x, yl, self.n.cc, *rows)
            self.n.send(ref, ref, ("gk", self.c) + key, way)

    def get(self, key, way, x, yl, rows, other=False):
        if rows[0] < rows[1]:
            self.n.recv(self.g(x, yl, self.n.cc1 if other else self.n.cc, *rows), ("gk", self.c) + key, way)

    def zero(self):
        n = self.n
        self.put(("y1",), "yl", n.xs[0], n.yl, self.first)
        for d, sign, w in ways:
            self.put(("x2", d), "x" + w, n.xs[0], n.yl, (0, NR))
        self.put(("c0",), "cc", n.xs[0], n.yl, (0, NR))
        self.put(("y2", 0), "yl", n.xs[0], n.yl, self.second)

    def one(self):
        n = self.n
        self.get(("y1",), "yl", n.xs[0], n.yl1, self.first)
        for d, sign, w in ways:
            self.put(("x1", d), "x" + w, n.xs[0], n.yl1, self.first)
        self.put(("c1",), "cc", n.xs[0], n.yl1, self.first)

    def two(self):
        n = self.n
        for d, sign, w in ways:
            src = n.xs[-sign]
            self.get(("x2", d), "x" + w, src, n.yl, (0, NR))
            self.put(("x2h", d), "x" + w, src, n.yl, halves(0, NR)[d])
            self.put(("y2", 1 + d), "yl", src, n.yl, self.second)
            self.put(("c2", d), "cc", src, n.yl, (0, NR))

    def three(self):
        n = self.n
        for d, sign, w in ways:
            src = n.xs[-sign]
            self.get(("x1", d), "x" + w, src, n.yl1, self.first)
            self.put(("x1h", d), "x" + w, src, n.yl1, halves(*self.first)[d])
            self.put(("c3", d), "cc", src, n.yl1, self.first)

    def four(self):
        n = self.n
        for d, sign, w in ways:
            self.get(("x2h", d), "x" + w, n.xs[2], n.yl, halves(0, NR)[d])
        self.put(("y2", 3), "yl", n.xs[2], n.yl, self.second)
        self.put(("c4",), "cc", n.xs[2], n.yl, (0, NR))

    def five(self):
        n = self.n
        for d, sign, w in ways:
            self.get(("x1h", d), "x" + w, n.xs[2], n.yl1, halves(*self.first)[d])
        self.put(("c5",), "cc", n.xs[2], n.yl1, self.first)

    def six(self):
        n = self.n
        for k, x in enumerate((n.xs[0], n.xs[-1], n.xs[1], n.xs[2])):
            self.get(("y2", k), "yl", x, n.yl1, self.second)
            self.put(("c6", k), "cc", x, n.yl1, self.second)

    def finish(self):
        n = self.n
        self.get(("c0",), "cc", n.xs[0], n.yl, (0, NR), True)
        self.get(("c1",), "cc", n.xs[0], n.yl1, self.first, True)
        for d, sign, w in ways:
            src = n.xs[-sign]
            self.get(("c2", d), "cc", src, n.yl, (0, NR), True)
            self.get(("c3", d), "cc", src, n.yl1, self.first, True)
        self.get(("c4",), "cc", n.xs[2], n.yl, (0, NR), True)
        self.get(("c5",), "cc", n.xs[2], n.yl1, self.first, True)
        for k, x in enumerate((n.xs[0], n.xs[-1], n.xs[1], n.xs[2])):
            self.get(("c6", k), "cc", x, n.yl1, self.second, True)


class ScatterJa:
    def __init__(self, net, N, bufs, c):
        self.n, self.N, self.c = net, N, c
        self.ry, self.first, self.rest, self.rf = bufs
        self.u, self.v, self.a = [{s: self.step(k, s) for s in range(1, 5)} for k in streams]

    def block(self, stream, z, lo, hi):
        col = self.n.yh1 if stream == "a" else self.n.yh
        return lambda: self.N.at[(self.c, col) + z + (pl.ds(lo, hi - lo),)]

    def land(self, stream, d, s):
        k = "uva".index(stream)
        if s == 1:
            return lambda: self.first.at[self.c, k, d]
        return lambda: self.rest.at[self.c, k, d, s - 2]

    def push(self, stream, s):
        for d, sign, w in ways:
            src = self.block(stream, self.n.zs[sign * (5 - s)], *rows_of(stream, d, s == 1))
            self.n.send(src, self.land(stream, d, s), ("rs", self.c, stream, d, s), "z" + w)

    def over(self, d):
        n, c = self.n, self.c
        src = lambda: self.N.at[(c, n.yh1) + n.zs[d] + (pl.ds(HR, HR),)]
        n.send(src, lambda: self.ry.at[c, d + 3], ("rsy", c, d), "yh")

    def over_got(self, d):
        n, c = self.n, self.c
        n.recv(lambda: self.ry.at[c, d + 3], ("rsy", c, d), "yh")
        accumulate(self.block("v", n.zs[d], *V)(), self.ry.at[c, d + 3])

    def start(self):
        self.over(4)
        self.push("a", 1)
        self.push("u", 1)
        for d in (3, -3, 2, -2, 1, -1, 0):
            self.over(d)

    def start_v(self):
        self.over_got(4)
        self.push("v", 1)

    def step(self, stream, s):
        def event():
            for d, sign, w in ways:
                if stream == "v" and (s < 4 or d == 0):
                    self.over_got(sign * (4 - s))
                land = self.land(stream, d, s)
                self.n.recv(land, ("rs", self.c, stream, d, s), "z" + w)
                accumulate(self.block(stream, self.n.zs[sign * (4 - s)], *rows_of(stream, d, s == 1))(), land())
            if s < 4:
                self.push(stream, s + 1)
            elif stream == "a":
                src = self.block("a", self.n.zs[0], *U)
                self.n.send(src, lambda: self.rf.at[self.c], ("rsf", self.c), "yh")

        return event

    def finish(self):
        n, c = self.n, self.c
        n.recv(lambda: self.rf.at[c], ("rsf", c), "yh")
        accumulate(self.block("u", n.zs[0], *U)(), self.rf.at[c])


def order(ag, rk, gk, rj, do, loop):
    return (
        do.prepare_left, do.left[0], do.entered, ag[0].start, do.left[1], do.prepare_right, do.loaded, (loop.right,
        (2, ag[0].u[1]), (2, ag[0].start_a), (3, ag[0].v[1]), (5, ag[0].u[2]), (7, ag[0].a[1]), (9, ag[0].v[2]),
        (10, ag[0].u[3])), ag[0].a[2], do.keep, ag[0].v[3], ag[0].u[4], ag[1].start, ag[0].a[3], ag[0].v[4],
        ag[1].u[1], ag[1].v[1], ag[1].start_a, ag[0].a[4], ag[1].u[2], ag[0].finish, (loop.turn_left[0], (1,
        ag[1].v[2]), (6, ag[1].a[1])), do.sent_left[0], (loop.product[0], (2, ag[1].u[3]), (4, ag[1].v[3]), (5,
        ag[1].a[2]), (7, ag[1].u[4])), ag[1].v[4], do.kept, (loop.turn_product[0], (3, ag[1].a[3])), rk[0].start,
        ag[1].a[4], ag[1].finish, (loop.turn_left[1],), do.sent_left[1], rk[0].one, do.sent_product[0],
        (loop.product[1], (5, rk[0].two)), rk[0].three, (loop.turn_product[1], (6, rk[0].four)), rk[1].start,
        rk[0].five, rk[1].one, do.sent_product[1], rk[0].six, do.rows[0], gk[0].zero, rk[1].two, rk[1].three,
        gk[0].two, rk[1].four, gk[0].one, rk[1].five, gk[0].four, gk[0].three, rk[1].six, do.rows[1], gk[1].zero,
        gk[0].five, gk[0].six, gk[0].finish, (loop.turn_grad[0], (3, gk[1].one), (4, gk[1].two)),
        (loop.left_product[0], (3, gk[1].three), (5, gk[1].four)), gk[1].five, (loop.turn_back[0], (7, gk[1].six)),
        rj[0].start, gk[1].finish, (loop.turn_grad[1], (6, rj[0].a[1]), (7, rj[0].start_v), (7, rj[0].u[1])),
        do.fetch_v, (loop.left_product[1], (3, rj[0].a[2]), (5, rj[0].v[1]), (6, rj[0].u[2])), do.fetch_s,
        (loop.turn_back[1], (1, rj[0].a[3]), (7, rj[0].v[2])), rj[1].start, rj[0].u[3], (loop.right_product, (4,
        rj[0].a[4]), (7, rj[1].start_v), (7, rj[0].v[3]), (9, rj[1].a[1]), (11, rj[1].u[1]), (14, rj[0].u[4])),
        do.fetched, (loop.right_pull, (1, rj[1].v[1]), (1, rj[0].v[4]), (3, rj[1].a[2]), (3, do.save[0]), (4,
        rj[1].u[2]), (6, rj[1].v[2]), (6, do.save[1]), (7, rj[1].a[3]), (7, rj[0].finish), (7, do.left_pull[0]), (7,
        rj[1].u[3]), (9, rj[1].v[3]), (9, do.save[2]), (10, rj[1].a[4])), rj[1].u[4], do.save[3], rj[1].v[4],
        rj[1].finish, do.left_pull[1],
    )


def kernel(
    pair, slab, gain, left_gate, left_value, right_gate, right_value, out_gain, out_weight, cot,
    update, grad_pair, grad_slab, s_kept, v_kept,
    xv, wl_up, wl_low, wlc_hi, wlc_lo, wr_up, wr_low, wrc_hi, wrc_lo,
    W, Rt, Lt, Gt, Hb, N, Q, x1a, x1b, y2, x2a, x2b, y1, ry, first, rest, rf, ss, rs, local,
):
    net = Net(ss, rs)
    entered = net.greet()
    load = pltpu.make_async_copy(pair, xv, local.at[0])
    load.start()
    G, Pn = W, N
    each = range(C)
    ag = [GatherJa(net, W, c) for c in each]
    rk = [ScatterKa(net, Pn, Q, (x1a, x1b, y2, x2a, x2b, y1), c) for c in each]
    gk = [GatherKa(net, G, c) for c in each]
    rj = [ScatterJa(net, N, (ry, first, rest, rf), c) for c in each]

    Wf = W.reshape(C * 16 * NR, B, 128)
    Nf = N.reshape(C * 16 * NR, B, 128)
    flat_R = Rt.reshape(128 * B, 128)
    flat_H = Hb.reshape(128 * HS, 128)
    flat_G = Gt.reshape(128 * 128, 128)
    flat_N = N.reshape(C * 16 * NR * B, 128)
    flat_W = W.reshape(C * 16 * NR * B, 128)
    factors = pl.ds(0, B * B)
    keep = [
        pltpu.make_async_copy(flat_G.at[factors], s_kept, local.at[5]),
        pltpu.make_async_copy(flat_N.at[factors], v_kept, local.at[6]),
    ]
    fetch = [
        pltpu.make_async_copy(s_kept, flat_R.at[factors], local.at[7]),
        pltpu.make_async_copy(v_kept, flat_W.at[factors], local.at[8]),
    ]

    def fetch_v():
        net.drain(*[("gk", c) for c in range(C)])
        fetch[1].start()

    K = 8

    def right(t):
        s, v = gates(normalise(xv[pl.ds(t * K, K)].reshape(K * B, 128))[0], wr_up, wr_low)
        part = pl.ds(t * K * B, K * B)
        flat_G[part, :] = s
        flat_N[part, :] = v
        made = s * v
        for u in range(K):
            tile = jnp.concatenate([made[u * B : (u + 1) * B], jnp.zeros((32, 128), f32)], 0).T
            flat_R[pl.ds(t * K + u, 128, stride=B), :] = tile

    def each_h(n, make):
        return 128 // n, lambda t: repeat(n, lambda u: make(t * n + u))

    def product(c):
        def make(h):
            Hb[h, c * CI : (c + 1) * CI, :B] = dot3(Lt[h, c * CI : (c + 1) * CI, :], Rt[h], NT)

        return each_h(16, make)

    def left_product(c):
        def make(h):
            turned = jnp.concatenate([Rt[h], jnp.zeros((32, 128), f32)], 0)
            Hb[h, c * CI : (c + 1) * CI, :] = dot3_wide(Gt[h, c * CI : (c + 1) * CI, :], turned)

        return each_h(16, make)

    def right_product(h):
        Hb[h, :B, :] = dot3_wide(Gt[h].T, Lt[h])[:B]

    def right_pull(t):
        grads = [flat_H[pl.ds(t * K + u, 128, stride=HS), :].T[:B] for u in range(K)]
        rows = xv[pl.ds(t * K, K)].reshape(K * B, 128)
        part = pl.ds(t * K * B, K * B)
        out = pull(rows, jnp.concatenate(grads, 0), flat_R[part, :], flat_W[part, :], wrc_hi, wrc_lo)
        xv[pl.ds(t * K, K)] = out.reshape(K, B, 128)

    def turn_in(dst, c):
        return CI // 8, lambda t: rows_in(Wf, dst, c * CI + t * 8, 8)

    def turn_out(c):
        return CI // 8, lambda t: rows_out(Hb, Nf, c * CI + t * 8, 8)

    loop = SimpleNamespace(
        right=(B // K, right),
        turn_left=[turn_in(Lt, c) for c in each],
        product=[product(c) for c in each],
        turn_product=[turn_out(c) for c in each],
        turn_grad=[turn_in(Gt, c) for c in each],
        left_product=[left_product(c) for c in each],
        turn_back=[turn_out(c) for c in each],
        right_product=each_h(8, right_product),
        right_pull=(B // K, right_pull),
    )

    def left(c):
        def step():
            own = forward(slab[c * NR : (c + 1) * NR].reshape(NR * B, 128), wl_up, wl_low)
            W[(c, net.yh) + net.zs[0]] = own.reshape(NR, B, 128)

        return step

    def rows(c):
        def step():
            mine = (c,) + net.xs[0] + (net.yl,)

            def one(u):
                r = c * NR + u
                normed, scale = normalise(Q[mine + (u,)])
                update[r] = dot3(normed * out_gain[...], out_weight[...])
                d = dot3(cot[r], out_weight[...], NT) * out_gain[...]
                G[mine + (net.cc, u)] = scale * (d - mean(d) - normed * mean(d * normed))

            repeat(NR, one)

        return step

    def left_pull(c):
        def step():
            grads = N[(c, net.yh) + net.zs[0]].reshape(NR * B, 128)
            mine = slab[c * NR : (c + 1) * NR].reshape(NR * B, 128)
            s, v = gates(normalise(mine)[0], wl_up, wl_low)
            out = pull(mine, grads, s, v, wlc_hi, wlc_lo)
            grad_slab[c * NR : (c + 1) * NR] = out.reshape(NR, B, 128)

        return step

    def save(k):
        part = pl.ds(k * (B // 4), B // 4)
        return pltpu.make_async_copy(xv.at[part], grad_pair.at[part], local.at[1 + k])

    do = SimpleNamespace(
        prepare_left=lambda: prepare(gain, left_gate, left_value, wl_up, wl_low, wlc_hi, wlc_lo),
        prepare_right=lambda: prepare(gain, right_gate, right_value, wr_up, wr_low, wrc_hi, wrc_lo),
        entered=entered,
        loaded=load.wait,
        keep=lambda: [copy.start() for copy in keep],
        kept=lambda: [copy.wait() for copy in keep],
        fetch_s=fetch[0].start,
        fetch_v=fetch_v,
        fetched=lambda: [copy.wait() for copy in fetch],
        left=[left(c) for c in each],
        rows=[rows(c) for c in each],
        left_pull=[left_pull(c) for c in each],
        save=[lambda k=k: save(k).start() for k in range(4)],
        sent_left=[lambda c=c: net.drain(("ag", c), ("agy", c)) for c in each],
        sent_product=[lambda c=c: net.drain(("core", c)) for c in each],
    )

    for entry in order(ag, rk, gk, rj, do, loop):
        if isinstance(entry, tuple):
            (n, body), *events = entry
            run(n, body, events)
        else:
            entry()
    net.drain()
    for k in range(4):
        save(k).wait()


def hand_over(update_in, pair_in, slab_in, update, pair, slab, held, into, out):
    parts = [(update_in, update, pl.ds(0, 8))]
    parts += [(pair_in.at[pl.ds(k, 12)], pair.at[pl.ds(k, 12)], pl.ds(8 + k, 12)) for k in range(0, B, 12)]
    parts += [(slab_in, slab, pl.ds(8 + B, 8))]
    loads = [pltpu.make_async_copy(a, held.at[p], into.at[k]) for k, (a, _, p) in enumerate(parts)]
    saves = [pltpu.make_async_copy(held.at[p], b, out.at[k]) for k, (_, b, p) in enumerate(parts)]
    for load in loads:
        load.start()
    for load, save in zip(loads, saves):
        load.wait()
        save.start()
    for save in saves:
        save.wait()


def shards(
    pair_map, slab_rows, norm_gain, left_gate, left_value, right_gate, right_value, out_gain, out_weight, cotangent
):
    S = jax.ShapeDtypeStruct
    M = pltpu.VMEM
    weights = [M((256, 256), bf16)] + [M((128, 256), bf16)] * 3
    made = pl.pallas_call(
        kernel,
        out_shape=[S((8,) + T, f32), S((B,) + T, f32), S((8,) + T, f32)] + [S((B * B, 128), f32)] * 2,
        in_specs=[HBM] + [VM] * 9,
        out_specs=[VM, HBM, VM, HBM, HBM],
        scratch_shapes=[M((B,) + T, f32)]
        + weights * 2
        + [
            M((C, 2, 2, 2, 2, NR) + T, f32),
            M((128, B, 128), f32),
            M((128, 128, 128), f32),
            M((128, 128, 128), f32),
            M((128, HS, 128), f32),
            M((C, 2, 2, 2, 2, NR) + T, f32),
            M((C, 2, 2, 2, NR) + T, f32),
            M((C, 2, YL, UP(max(KR))) + T, f32),
            M((C, 2, YL, max(KR)) + T, f32),
            M((C, 2, 2, max(NR - min(KR), 1)) + T, f32),
            M((C, 2, max(UP(NR - min(KR)), 1)) + T, f32),
            M((C, 2, max(NR - min(KR), 1)) + T, f32),
            M((C, max(KR)) + T, f32),
            M((C, Z, HR) + T, f32),
            M((C, 3, 2, QR) + T, f32),
            M((C, 3, 2, 3, HR) + T, f32),
            M((C, HR) + T, f32),
            pltpu.SemaphoreType.DMA((240,)),
            pltpu.SemaphoreType.DMA((240,)),
            pltpu.SemaphoreType.DMA((9,)),
        ],
        compiler_params=pltpu.CompilerParams(collective_id=1, has_side_effects=True, vmem_limit_bytes=63 * MIB + MIB // 2),
        name="triangle",
    )(
        pair_map, slab_rows, norm_gain.reshape(1, 128), left_gate, left_value, right_gate, right_value,
        out_gain.reshape(1, 128), out_weight, cotangent,
    )
    return pl.pallas_call(
        hand_over,
        out_shape=[S((8,) + T, f32), S((B,) + T, f32), S((8,) + T, f32)],
        in_specs=[HBM] * 3,
        out_specs=[HBM] * 3,
        scratch_shapes=[M((B + 16,) + T, f32), pltpu.SemaphoreType.DMA((10,)), pltpu.SemaphoreType.DMA((10,))],
        compiler_params=pltpu.CompilerParams(vmem_limit_bytes=16 * MIB),
        name="hand_over",
    )(*made[:3])


def solution(mesh):
    in_specs = (
        P("ja", "ka", None),
        P("ja", "ka", None),
        P(),
        P(),
        P(),
        P(),
        P(),
        P(),
        P(),
        P("ka", "ja", None),
    )
    out_specs = (P("ka", "ja", None), P("ja", "ka", None), P("ja", "ka", None))
    return jax.shard_map(shards, mesh=mesh, in_specs=in_specs, out_specs=out_specs, check_vma=False)
```

```python
from types import SimpleNamespace

import jax
import jax.numpy as jnp
from jax import lax
from jax.experimental import pallas as pl
from jax.experimental.pallas import tpu as pltpu
from jax.sharding import PartitionSpec as P

f32, bf16 = jnp.float32, jnp.bfloat16
norm_eps = 1e-05

YH, Z, X, YL, CORE = 2, 8, 4, 2, 2
C = 2
NR = 8 // C
HR, QR = NR // 2, NR // 4
KR = (2, 2)
KG = (2, 2)
CI = 16 * NR
B = 96
HS = 136
T = (B, 128)
MIB = 2**20
MESH = pl.DeviceIdType.MESH
NT = (((1,), (1,)), ((), ()))
NN = (((1,), (0,)), ((), ()))
VM = pl.BlockSpec(memory_space=pltpu.VMEM)
HBM = pl.BlockSpec(memory_space=pl.ANY)


def split(values):
    hi = values.astype(bf16)
    return hi, (values - hi.astype(f32)).astype(bf16)


def dot(a, b, dims=NN):
    return lax.dot_general(a, b, dims, preferred_element_type=f32)


def dot3(a, b, dims=NN):
    a_hi, a_lo = split(a)
    b_hi, b_lo = split(b)
    both = dot(jnp.concatenate([a_hi, a_lo], 1), jnp.concatenate([b_hi, b_hi], dims[0][1][0]), dims)
    return both + dot(a_hi, b_lo, dims)


def dot3_wide(a, b):
    a_hi, a_lo = split(a)
    b_hi, b_lo = split(b)
    upper = jnp.concatenate([b_hi, b_lo], 1)
    lower = jnp.concatenate([b_hi, jnp.zeros_like(b_lo)], 1)
    both = dot(jnp.concatenate([a_hi, a_lo], 1), jnp.concatenate([upper, lower], 0))
    return both[:, : b.shape[1]] + both[:, b.shape[1] :]


def mean(values):
    return jnp.mean(values, axis=-1, keepdims=True)


def normalise(values):
    center = values - mean(values)
    scale = lax.rsqrt(mean(center * center) + norm_eps)
    return center * scale, scale


def prepare(gain, gate, value, w_up, w_low, wc_hi, wc_lo):
    column = jnp.broadcast_to(gain[...], (128, 128)).T
    folded = jnp.concatenate([gate[...] * column, value[...] * column], 1)
    hi, lo = split(folded)
    w_up[:128] = hi
    w_up[128:] = hi
    w_low[...] = lo
    hi, lo = split(folded - jnp.mean(folded, axis=0, keepdims=True))
    wc_hi[...] = hi
    wc_lo[...] = lo


def gates(normed, w_up, w_low):
    hi, lo = split(normed)
    both = dot(jnp.concatenate([hi, lo], 1), w_up[...]) + dot(hi, w_low[...])
    return 1.0 / (1.0 + jnp.exp(-both[:, :128])), both[:, 128:]


def forward(values, w_up, w_low):
    s, v = gates(normalise(values)[0], w_up, w_low)
    return s * v


def pull(values, grad, s, v, wc_hi, wc_lo):
    normed, scale = normalise(values)
    d_value = grad * s
    d_gate = d_value * v * (1.0 - s)
    hi, lo = split(jnp.concatenate([d_gate, d_value], 1))
    d = dot(hi, wc_hi[...], NT) + dot(lo, wc_hi[...], NT) + dot(hi, wc_lo[...], NT)
    return scale * (d - normed * mean(d * normed))


def accumulate(dst, src):
    dims = src.shape[:-2]
    if not dims:
        dst[...] = dst[...] + src[...]
        return

    def step(i, _):
        accumulate(dst.at[i], src.at[i])
        return 0

    lax.fori_loop(0, dims[0], step, 0, unroll=True)


def repeat(n, body):
    def step(i, _):
        body(i)
        return 0

    lax.fori_loop(0, n, step, 0, unroll=True)


def run(n, body, events=()):
    def step(t, _):
        for at, event in events:
            pl.when(t == at)(event)
        body(t)
        return 0

    lax.fori_loop(0, n, step, 0)


def rows_in(src, dst, first, n):
    flat = dst.reshape(dst.shape[0] * dst.shape[1], 128)

    def body(u):
        row = first + u
        tile = jnp.concatenate([src[row], jnp.zeros((32, 128), f32)], 0).T
        flat[pl.ds(row, 128, stride=dst.shape[1]), :] = tile

    repeat(n, body)


def rows_out(src, dst, first, n):
    flat = src.reshape(src.shape[0] * src.shape[1], 128)

    def body(u):
        row = first + u
        dst[row] = flat[pl.ds(row, 128, stride=src.shape[1]), :].T[:B]

    repeat(n, body)


class Net:
    def __init__(self, ss, rs):
        self.ss, self.rs = ss, rs
        self.keys, self.sent = {}, []
        ja, ka = lax.axis_index("ja"), lax.axis_index("ka")
        self.yh, self.z = ja // 8, ja % 8
        self.x, self.yl, self.cc = ka // 4, (ka // 2) % 2, ka % 2
        self.yh1, self.yl1, self.cc1 = 1 - self.yh, 1 - self.yl, 1 - self.cc
        self.zs = {d: by_z((self.z + d + 8) % 8) for d in range(-4, 5)}
        z_at = {d: (self.z + d + 8) % 8 for d in (-1, 1)}
        self.xs = {d: by_x((self.x + d + 4) % 4) for d in range(-2, 3)}
        x_at = {d: (self.x + d + 4) % 4 for d in (-1, 1)}
        self.to = {
            "z+": (self.yh * 8 + z_at[1], ka),
            "z-": (self.yh * 8 + z_at[-1], ka),
            "yh": (self.yh1 * 8 + self.z, ka),
            "x+": (ja, x_at[1] * 4 + ka % 4),
            "x-": (ja, x_at[-1] * 4 + ka % 4),
            "yl": (ja, self.x * 4 + self.yl1 * 2 + self.cc),
            "cc": (ja, self.x * 4 + self.yl * 2 + self.cc1),
        }

    def greet(self):
        barrier = pltpu.get_barrier_semaphore()
        for dev in self.to.values():
            pl.semaphore_signal(barrier, inc=1, device_id=dev, device_id_type=MESH)
        return lambda: pl.semaphore_wait(barrier, len(self.to))

    def copy(self, src, dst, key, way):
        k = self.keys.setdefault(key, len(self.keys))
        return pltpu.make_async_remote_copy(
            src_ref=src(),
            dst_ref=dst(),
            send_sem=self.ss.at[k],
            recv_sem=self.rs.at[k],
            device_id=self.to[way],
            device_id_type=MESH,
        )

    def send(self, src, dst, key, way):
        self.copy(src, dst, key, way).start()
        self.sent.append((src, dst, key, way))

    def recv(self, dst, key, way):
        self.copy(dst, dst, key, way).wait_recv()

    def drain(self, *kinds):
        for entry in [e for e in self.sent if not kinds or e[2][:2] in kinds]:
            self.copy(*entry).wait_send()
            self.sent.remove(entry)


ways = ((0, 1, "+"), (1, -1, "-"))


def by_z(z):
    return z // 4, (z // 2) % 2, z % 2


def by_x(x):
    return x // 2, x % 2


def UP(rows):
    return (rows + 1) // 2


def halves(lo, hi):
    mid = (lo + hi) // 2
    return (lo, mid), (mid, hi)


U, V = (0, HR), (HR, NR)
streams = {"u": U, "v": V, "a": U}


def rows_of(stream, d, end):
    return halves(*streams[stream])[d] if end else streams[stream]


class GatherJa:
    def __init__(self, net, W, c):
        self.n, self.W, self.c = net, W, c
        self.u, self.v, self.a = [{s: self.step(k, s) for s in range(1, 5)} for k in streams]

    def at(self, yh, z, lo, hi):
        return lambda: self.W.at[(self.c, yh) + z + (pl.ds(lo, hi - lo),)]

    def piece(self, stream, d, z, s):
        return self.at(self.n.yh1 if stream == "a" else self.n.yh, z, *rows_of(stream, d, s == 4))

    def hop(self, stream, s):
        for d, sign, w in ways:
            ref = self.piece(stream, d, self.n.zs[-sign * (s - 1)], s)
            self.n.send(ref, ref, ("ag", self.c, stream, d, s), "z" + w)

    def over(self, d, rows):
        ref = self.at(self.n.yh, self.n.zs[d], *rows)
        self.n.send(ref, ref, ("agy", self.c, d, rows), "yh")

    def over_got(self, d, rows):
        self.n.recv(self.at(self.n.yh1, self.n.zs[d], *rows), ("agy", self.c, d, rows), "yh")

    def start(self):
        self.hop("u", 1)
        self.over(0, U)
        self.hop("v", 1)
        self.over(0, V)

    def start_a(self):
        self.over_got(0, U)
        self.hop("a", 1)

    def step(self, stream, s):
        def event():
            for d, sign, w in ways:
                ref = self.piece(stream, d, self.n.zs[-sign * s], s)
                self.n.recv(ref, ("ag", self.c, stream, d, s), "z" + w)
            if s < 4:
                self.hop(stream, s + 1)
            if stream == "v":
                for d in (-s, s) if s < 4 else (4,):
                    self.over(d, V)

        return event

    def finish(self):
        for d in (0, -1, 1, -2, 2, -3, 3, 4):
            self.over_got(d, V)


class ScatterKa:
    def __init__(self, net, Pn, Q, bufs, c):
        self.n, self.Pn, self.Q, self.c = net, Pn, Q, c
        self.x1a, self.x1b, self.y2, self.x2a, self.x2b, self.y1 = bufs
        self.k = KR[c]
        self.first, self.second = (0, self.k), (self.k, NR)

    def q(self, x, yl, lo, hi):
        return lambda: self.Q.at[(self.c,) + x + (slice(None) if yl is None else yl, pl.ds(lo, hi - lo))]

    def land(self, buf, rows, *where):
        return lambda: buf.at[(self.c,) + where + (pl.ds(0, rows[1] - rows[0]),)]

    def halves_of_core(self):
        return [rows for rows in (self.second, self.first) if rows[0] < rows[1]]

    def start(self):
        n, c = self.n, self.c
        for k, (lo, hi) in enumerate(self.halves_of_core()):
            part = pl.ds(lo, hi - lo)
            src = lambda part=part: self.Pn.at[c, :, :, :, n.cc1, part]
            n.send(src, lambda part=part: self.Q.at[c, :, :, :, part], ("core", c, k), "cc")

    def far(self, buf, key, rows, yl):
        for d, sign, w in ways:
            part = halves(*rows)[d]
            if part[0] < part[1]:
                where = (d, slice(None)) if yl is None else (d,)
                self.n.send(self.q(self.n.xs[2], yl, *part), self.land(buf, part, *where), (key, self.c, d), "x" + w)

    def near(self, far, far_key, buf, key, rows, yl):
        for d, sign, w in ways:
            part = halves(*rows)[d]
            where = (d, slice(None)) if yl is None else (d,)
            if part[0] < part[1]:
                land = self.land(far, part, *where)
                self.n.recv(land, (far_key, self.c, d), "x" + w)
                accumulate(self.q(self.n.xs[sign], yl, *part)(), land())
            self.n.send(self.q(self.n.xs[sign], yl, *rows), self.land(buf, rows, *where), (key, self.c, d), "x" + w)

    def last(self, buf, key, rows, yl):
        for d, sign, w in ways:
            land = self.land(buf, rows, *((d, slice(None)) if yl is None else (d,)))
            self.n.recv(land, (key, self.c, d), "x" + w)
            accumulate(self.q(self.n.xs[0], yl, *rows)(), land())

    def one(self):
        n, c = self.n, self.c
        for k, (lo, hi) in enumerate(self.halves_of_core()):
            part = pl.ds(lo, hi - lo)
            n.recv(lambda: self.Q.at[c, :, :, :, part], ("core", c, k), "cc")
            accumulate(self.Q.at[c, :, :, :, part], self.Pn.at[c, :, :, :, n.cc, part])
            if lo > 0:
                land = self.land(self.y2, self.second, slice(None), slice(None))
                n.send(lambda part=part: self.Q.at[c, :, :, n.yl1, part], land, ("y2", c), "yl")
        self.far(self.x1a, "x1a", self.first, None)

    def two(self):
        self.near(self.x1a, "x1a", self.x1b, "x1b", self.first, None)

    def three(self):
        n, c = self.n, self.c
        if self.k < NR:
            land = self.land(self.y2, self.second, slice(None), slice(None))
            n.recv(land, ("y2", c), "yl")
            accumulate(self.Q.at[c, :, :, n.yl, pl.ds(self.k, NR - self.k)], land())
            self.far(self.x2a, "x2a", self.second, n.yl)

    def four(self):
        n, c = self.n, self.c
        self.last(self.x1b, "x1b", self.first, None)
        n.send(self.q(n.xs[0], n.yl1, *self.first), self.land(self.y1, self.first), ("y1", c), "yl")

    def five(self):
        if self.k < NR:
            self.near(self.x2a, "x2a", self.x2b, "x2b", self.second, self.n.yl)

    def six(self):
        n, c = self.n, self.c
        n.recv(self.land(self.y1, self.first), ("y1", c), "yl")
        accumulate(self.q(n.xs[0], n.yl, *self.first)(), self.land(self.y1, self.first)())
        if self.k < NR:
            self.last(self.x2b, "x2b", self.second, n.yl)


class GatherKa:
    def __init__(self, net, G, c):
        self.n, self.G, self.c = net, G, c
        self.k = KG[c]
        self.first, self.second = (0, self.k), (self.k, NR)
        self.mixed = self.k < NR

    def g(self, x, yl, core, lo, hi):
        return lambda: self.G.at[(self.c,) + x + (yl, core, pl.ds(lo, hi - lo))]

    def put(self, key, way, x, yl, rows):
        if rows[0] < rows[1]:
            ref = self.g(x, yl, self.n.cc, *rows)
            self.n.send(ref, ref, ("gk", self.c) + key, way)

    def get(self, key, way, x, yl, rows, other=False):
        if rows[0] < rows[1]:
            self.n.recv(self.g(x, yl, self.n.cc1 if other else self.n.cc, *rows), ("gk", self.c) + key, way)

    def zero(self):
        n = self.n
        self.put(("y1",), "yl", n.xs[0], n.yl, self.first)
        for d, sign, w in ways:
            self.put(("x2", d), "x" + w, n.xs[0], n.yl, (0, NR))
        self.put(("c0",), "cc", n.xs[0], n.yl, (0, NR))
        self.put(("y2", 0), "yl", n.xs[0], n.yl, self.second)

    def one(self):
        n = self.n
        self.get(("y1",), "yl", n.xs[0], n.yl1, self.first)
        for d, sign, w in ways:
            self.put(("x1", d), "x" + w, n.xs[0], n.yl1, self.first)
        self.put(("c1",), "cc", n.xs[0], n.yl1, self.first)

    def two(self):
        n = self.n
        for d, sign, w in ways:
            src = n.xs[-sign]
            self.get(("x2", d), "x" + w, src, n.yl, (0, NR))
            self.put(("x2h", d), "x" + w, src, n.yl, halves(0, NR)[d])
            self.put(("y2", 1 + d), "yl", src, n.yl, self.second)
            self.put(("c2", d), "cc", src, n.yl, (0, NR))

    def three(self):
        n = self.n
        for d, sign, w in ways:
            src = n.xs[-sign]
            self.get(("x1", d), "x" + w, src, n.yl1, self.first)
            self.put(("x1h", d), "x" + w, src, n.yl1, halves(*self.first)[d])
            self.put(("c3", d), "cc", src, n.yl1, self.first)

    def four(self):
        n = self.n
        for d, sign, w in ways:
            self.get(("x2h", d), "x" + w, n.xs[2], n.yl, halves(0, NR)[d])
        self.put(("y2", 3), "yl", n.xs[2], n.yl, self.second)
        self.put(("c4",), "cc", n.xs[2], n.yl, (0, NR))

    def five(self):
        n = self.n
        for d, sign, w in ways:
            self.get(("x1h", d), "x" + w, n.xs[2], n.yl1, halves(*self.first)[d])
        self.put(("c5",), "cc", n.xs[2], n.yl1, self.first)

    def six(self):
        n = self.n
        for k, x in enumerate((n.xs[0], n.xs[-1], n.xs[1], n.xs[2])):
            self.get(("y2", k), "yl", x, n.yl1, self.second)
            self.put(("c6", k), "cc", x, n.yl1, self.second)

    def finish(self):
        n = self.n
        self.get(("c0",), "cc", n.xs[0], n.yl, (0, NR), True)
        self.get(("c1",), "cc", n.xs[0], n.yl1, self.first, True)
        for d, sign, w in ways:
            src = n.xs[-sign]
            self.get(("c2", d), "cc", src, n.yl, (0, NR), True)
            self.get(("c3", d), "cc", src, n.yl1, self.first, True)
        self.get(("c4",), "cc", n.xs[2], n.yl, (0, NR), True)
        self.get(("c5",), "cc", n.xs[2], n.yl1, self.first, True)
        for k, x in enumerate((n.xs[0], n.xs[-1], n.xs[1], n.xs[2])):
            self.get(("c6", k), "cc", x, n.yl1, self.second, True)


class ScatterJa:
    def __init__(self, net, N, bufs, c):
        self.n, self.N, self.c = net, N, c
        self.ry, self.first, self.rest, self.rf = bufs
        self.u, self.v, self.a = [{s: self.step(k, s) for s in range(1, 5)} for k in streams]

    def block(self, stream, z, lo, hi):
        col = self.n.yh1 if stream == "a" else self.n.yh
        return lambda: self.N.at[(self.c, col) + z + (pl.ds(lo, hi - lo),)]

    def land(self, stream, d, s):
        k = "uva".index(stream)
        if s == 1:
            return lambda: self.first.at[self.c, k, d]
        return lambda: self.rest.at[self.c, k, d, s - 2]

    def push(self, stream, s):
        for d, sign, w in ways:
            src = self.block(stream, self.n.zs[sign * (5 - s)], *rows_of(stream, d, s == 1))
            self.n.send(src, self.land(stream, d, s), ("rs", self.c, stream, d, s), "z" + w)

    def over(self, d):
        n, c = self.n, self.c
        src = lambda: self.N.at[(c, n.yh1) + n.zs[d] + (pl.ds(HR, HR),)]
        n.send(src, lambda: self.ry.at[c, d + 3], ("rsy", c, d), "yh")

    def over_got(self, d):
        n, c = self.n, self.c
        n.recv(lambda: self.ry.at[c, d + 3], ("rsy", c, d), "yh")
        accumulate(self.block("v", n.zs[d], *V)(), self.ry.at[c, d + 3])

    def start(self):
        self.over(4)
        self.push("a", 1)
        self.push("u", 1)
        for d in (3, -3, 2, -2, 1, -1, 0):
            self.over(d)

    def start_v(self):
        self.over_got(4)
        self.push("v", 1)

    def step(self, stream, s):
        def event():
            for d, sign, w in ways:
                if stream == "v" and (s < 4 or d == 0):
                    self.over_got(sign * (4 - s))
                land = self.land(stream, d, s)
                self.n.recv(land, ("rs", self.c, stream, d, s), "z" + w)
                accumulate(self.block(stream, self.n.zs[sign * (4 - s)], *rows_of(stream, d, s == 1))(), land())
            if s < 4:
                self.push(stream, s + 1)
            elif stream == "a":
                src = self.block("a", self.n.zs[0], *U)
                self.n.send(src, lambda: self.rf.at[self.c], ("rsf", self.c), "yh")

        return event

    def finish(self):
        n, c = self.n, self.c
        n.recv(lambda: self.rf.at[c], ("rsf", c), "yh")
        accumulate(self.block("u", n.zs[0], *U)(), self.rf.at[c])


def order(ag, rk, gk, rj, do, loop):
    return (
        do.prepare_left, do.left[0], do.entered, ag[0].start, do.left[1], do.prepare_right, do.loaded, (loop.right,
        (3, ag[0].u[1]), (3, ag[0].start_a), (5, ag[0].v[1]), (7, ag[0].u[2]), (9, ag[0].a[1]), (11, ag[0].v[2])),
        do.keep, ag[0].u[3], ag[0].a[2], ag[0].v[3], ag[0].u[4], ag[1].start, ag[0].a[3], ag[0].v[4], ag[1].u[1],
        ag[1].v[1], ag[1].start_a, ag[0].a[4], ag[1].u[2], ag[1].v[2], ag[0].finish, (loop.turn_left[0], (5,
        ag[1].a[1])), do.sent_left[0], (loop.product[0], (1, ag[1].u[3]), (4, ag[1].v[3]), (6, ag[1].a[2]), (7,
        ag[1].u[4])), do.kept, (loop.turn_product[0], (1, ag[1].v[4])), rk[0].start, ag[1].a[3], ag[1].a[4],
        ag[1].finish, rk[0].one, do.sent_product[0], (loop.turn_left[1],), do.sent_left[1], (loop.product[1], (3,
        rk[0].two), (7, rk[0].three)), (loop.turn_product[1], (5, rk[0].four)), rk[1].start, rk[0].five, rk[1].one,
        do.sent_product[1], rk[0].six, do.rows[0], gk[0].zero, rk[1].two, rk[1].three, gk[0].two, rk[1].four,
        gk[0].one, rk[1].five, gk[0].four, gk[0].three, rk[1].six, do.rows[1], gk[1].zero, gk[0].five, gk[0].six,
        gk[0].finish, (loop.turn_grad[0], (5, gk[1].one), (7, gk[1].two)), (loop.left_product[0], (5, gk[1].three)),
        gk[1].four, (loop.turn_back[0], (7, gk[1].five)), rj[0].start, gk[1].six, rj[0].a[1], gk[1].finish,
        rj[0].start_v, rj[0].u[1], (loop.turn_grad[1],), do.fetch_v, (loop.left_product[1], (1, rj[0].a[2]), (3,
        rj[0].v[1]), (5, rj[0].u[2])), rj[0].a[3], do.fetch_s, (loop.turn_back[1], (5, rj[0].v[2])), rj[1].start,
        rj[0].u[3], (loop.right_product, (4, rj[0].a[4]), (8, rj[0].v[3]), (8, rj[1].start_v), (10, rj[1].a[1]),
        (12, rj[1].u[1]), (15, rj[0].u[4])), do.fetched, (loop.right_pull, (2, rj[0].v[4]), (3, rj[1].v[1]), (3,
        do.save[0]), (4, rj[1].a[2]), (6, rj[1].u[2]), (6, do.save[1]), (7, rj[1].v[2]), (9, rj[1].a[3]), (9,
        do.save[2]), (10, rj[0].finish), (10, rj[1].u[3]), (10, do.left_pull[0]), (11, rj[1].v[3])), rj[1].a[4],
        do.save[3], rj[1].u[4], rj[1].v[4], rj[1].finish, do.left_pull[1],
    )


def kernel(
    pair, slab, gain, left_gate, left_value, right_gate, right_value, out_gain, out_weight, cot,
    update, grad_pair, grad_slab, s_kept, v_kept,
    xv, wl_up, wl_low, wlc_hi, wlc_lo, wr_up, wr_low, wrc_hi, wrc_lo,
    W, Rt, Lt, Gt, Hb, N, Q, x1a, x1b, y2, x2a, x2b, y1, ry, first, rest, rf, ss, rs, local,
):
    net = Net(ss, rs)
    entered = net.greet()
    load = pltpu.make_async_copy(pair, xv, local.at[0])
    load.start()
    G, Pn = W, N
    each = range(C)
    ag = [GatherJa(net, W, c) for c in each]
    rk = [ScatterKa(net, Pn, Q, (x1a, x1b, y2, x2a, x2b, y1), c) for c in each]
    gk = [GatherKa(net, G, c) for c in each]
    rj = [ScatterJa(net, N, (ry, first, rest, rf), c) for c in each]

    Wf = W.reshape(C * 16 * NR, B, 128)
    Nf = N.reshape(C * 16 * NR, B, 128)
    flat_R = Rt.reshape(128 * B, 128)
    flat_H = Hb.reshape(128 * HS, 128)
    flat_G = Gt.reshape(128 * 128, 128)
    flat_N = N.reshape(C * 16 * NR * B, 128)
    flat_W = W.reshape(C * 16 * NR * B, 128)
    factors = pl.ds(0, B * B)
    keep = [
        pltpu.make_async_copy(flat_G.at[factors], s_kept, local.at[5]),
        pltpu.make_async_copy(flat_N.at[factors], v_kept, local.at[6]),
    ]
    fetch = [
        pltpu.make_async_copy(s_kept, flat_R.at[factors], local.at[7]),
        pltpu.make_async_copy(v_kept, flat_W.at[factors], local.at[8]),
    ]

    def fetch_v():
        net.drain(*[("gk", c) for c in range(C)])
        fetch[1].start()

    K = 8

    def right(t):
        s, v = gates(normalise(xv[pl.ds(t * K, K)].reshape(K * B, 128))[0], wr_up, wr_low)
        part = pl.ds(t * K * B, K * B)
        flat_G[part, :] = s
        flat_N[part, :] = v
        made = s * v
        for u in range(K):
            tile = jnp.concatenate([made[u * B : (u + 1) * B], jnp.zeros((32, 128), f32)], 0).T
            flat_R[pl.ds(t * K + u, 128, stride=B), :] = tile

    def each_h(n, make):
        return 128 // n, lambda t: repeat(n, lambda u: make(t * n + u))

    def product(c):
        def make(h):
            Hb[h, c * CI : (c + 1) * CI, :B] = dot3(Lt[h, c * CI : (c + 1) * CI, :], Rt[h], NT)

        return each_h(16, make)

    def left_product(c):
        def make(h):
            turned = jnp.concatenate([Rt[h], jnp.zeros((32, 128), f32)], 0)
            Hb[h, c * CI : (c + 1) * CI, :] = dot3_wide(Gt[h, c * CI : (c + 1) * CI, :], turned)

        return each_h(16, make)

    def right_product(h):
        Hb[h, :B, :] = dot3_wide(Gt[h].T, Lt[h])[:B]

    def right_pull(t):
        grads = [flat_H[pl.ds(t * K + u, 128, stride=HS), :].T[:B] for u in range(K)]
        rows = xv[pl.ds(t * K, K)].reshape(K * B, 128)
        part = pl.ds(t * K * B, K * B)
        out = pull(rows, jnp.concatenate(grads, 0), flat_R[part, :], flat_W[part, :], wrc_hi, wrc_lo)
        xv[pl.ds(t * K, K)] = out.reshape(K, B, 128)

    def turn_in(dst, c):
        return CI // 8, lambda t: rows_in(Wf, dst, c * CI + t * 8, 8)

    def turn_out(c):
        return CI // 8, lambda t: rows_out(Hb, Nf, c * CI + t * 8, 8)

    loop = SimpleNamespace(
        right=(B // K, right),
        turn_left=[turn_in(Lt, c) for c in each],
        product=[product(c) for c in each],
        turn_product=[turn_out(c) for c in each],
        turn_grad=[turn_in(Gt, c) for c in each],
        left_product=[left_product(c) for c in each],
        turn_back=[turn_out(c) for c in each],
        right_product=each_h(8, right_product),
        right_pull=(B // K, right_pull),
    )

    def left(c):
        def step():
            own = forward(slab[c * NR : (c + 1) * NR].reshape(NR * B, 128), wl_up, wl_low)
            W[(c, net.yh) + net.zs[0]] = own.reshape(NR, B, 128)

        return step

    def rows(c):
        def step():
            mine = (c,) + net.xs[0] + (net.yl,)

            def one(u):
                r = c * NR + u
                normed, scale = normalise(Q[mine + (u,)])
                update[r] = dot3(normed * out_gain[...], out_weight[...])
                d = dot3(cot[r], out_weight[...], NT) * out_gain[...]
                G[mine + (net.cc, u)] = scale * (d - mean(d) - normed * mean(d * normed))

            repeat(NR, one)

        return step

    def left_pull(c):
        def step():
            grads = N[(c, net.yh) + net.zs[0]].reshape(NR * B, 128)
            mine = slab[c * NR : (c + 1) * NR].reshape(NR * B, 128)
            s, v = gates(normalise(mine)[0], wl_up, wl_low)
            out = pull(mine, grads, s, v, wlc_hi, wlc_lo)
            grad_slab[c * NR : (c + 1) * NR] = out.reshape(NR, B, 128)

        return step

    def save(k):
        part = pl.ds(k * (B // 4), B // 4)
        return pltpu.make_async_copy(xv.at[part], grad_pair.at[part], local.at[1 + k])

    do = SimpleNamespace(
        prepare_left=lambda: prepare(gain, left_gate, left_value, wl_up, wl_low, wlc_hi, wlc_lo),
        prepare_right=lambda: prepare(gain, right_gate, right_value, wr_up, wr_low, wrc_hi, wrc_lo),
        entered=entered,
        loaded=load.wait,
        keep=lambda: [copy.start() for copy in keep],
        kept=lambda: [copy.wait() for copy in keep],
        fetch_s=fetch[0].start,
        fetch_v=fetch_v,
        fetched=lambda: [copy.wait() for copy in fetch],
        left=[left(c) for c in each],
        rows=[rows(c) for c in each],
        left_pull=[left_pull(c) for c in each],
        save=[lambda k=k: save(k).start() for k in range(4)],
        sent_left=[lambda c=c: net.drain(("ag", c), ("agy", c)) for c in each],
        sent_product=[lambda c=c: net.drain(("core", c)) for c in each],
    )

    for entry in order(ag, rk, gk, rj, do, loop):
        if isinstance(entry, tuple):
            (n, body), *events = entry
            run(n, body, events)
        else:
            entry()
    net.drain()
    for k in range(4):
        save(k).wait()


def hand_over(update_in, pair_in, slab_in, update, pair, slab, held, into, out):
    parts = [(update_in, update, pl.ds(0, 8))]
    parts += [(pair_in.at[pl.ds(k, 12)], pair.at[pl.ds(k, 12)], pl.ds(8 + k, 12)) for k in range(0, B, 12)]
    parts += [(slab_in, slab, pl.ds(8 + B, 8))]
    loads = [pltpu.make_async_copy(a, held.at[p], into.at[k]) for k, (a, _, p) in enumerate(parts)]
    saves = [pltpu.make_async_copy(held.at[p], b, out.at[k]) for k, (_, b, p) in enumerate(parts)]
    for load in loads:
        load.start()
    for load, save in zip(loads, saves):
        load.wait()
        save.start()
    for save in saves:
        save.wait()


def shards(
    pair_map, slab_rows, norm_gain, left_gate, left_value, right_gate, right_value, out_gain, out_weight, cotangent
):
    S = jax.ShapeDtypeStruct
    M = pltpu.VMEM
    weights = [M((256, 256), bf16)] + [M((128, 256), bf16)] * 3
    made = pl.pallas_call(
        kernel,
        out_shape=[S((8,) + T, f32), S((B,) + T, f32), S((8,) + T, f32)] + [S((B * B, 128), f32)] * 2,
        in_specs=[HBM] + [VM] * 9,
        out_specs=[VM, HBM, VM, HBM, HBM],
        scratch_shapes=[M((B,) + T, f32)]
        + weights * 2
        + [
            M((C, 2, 2, 2, 2, NR) + T, f32),
            M((128, B, 128), f32),
            M((128, 128, 128), f32),
            M((128, 128, 128), f32),
            M((128, HS, 128), f32),
            M((C, 2, 2, 2, 2, NR) + T, f32),
            M((C, 2, 2, 2, NR) + T, f32),
            M((C, 2, YL, UP(max(KR))) + T, f32),
            M((C, 2, YL, max(KR)) + T, f32),
            M((C, 2, 2, max(NR - min(KR), 1)) + T, f32),
            M((C, 2, max(UP(NR - min(KR)), 1)) + T, f32),
            M((C, 2, max(NR - min(KR), 1)) + T, f32),
            M((C, max(KR)) + T, f32),
            M((C, Z, HR) + T, f32),
            M((C, 3, 2, QR) + T, f32),
            M((C, 3, 2, 3, HR) + T, f32),
            M((C, HR) + T, f32),
            pltpu.SemaphoreType.DMA((240,)),
            pltpu.SemaphoreType.DMA((240,)),
            pltpu.SemaphoreType.DMA((9,)),
        ],
        compiler_params=pltpu.CompilerParams(collective_id=1, has_side_effects=True, vmem_limit_bytes=63 * MIB + MIB // 2),
        name="triangle",
    )(
        pair_map, slab_rows, norm_gain.reshape(1, 128), left_gate, left_value, right_gate, right_value,
        out_gain.reshape(1, 128), out_weight, cotangent,
    )
    return pl.pallas_call(
        hand_over,
        out_shape=[S((8,) + T, f32), S((B,) + T, f32), S((8,) + T, f32)],
        in_specs=[HBM] * 3,
        out_specs=[HBM] * 3,
        scratch_shapes=[M((B + 16,) + T, f32), pltpu.SemaphoreType.DMA((10,)), pltpu.SemaphoreType.DMA((10,))],
        compiler_params=pltpu.CompilerParams(vmem_limit_bytes=62 * MIB),
        name="hand_over",
    )(*made[:3])


def solution(mesh):
    in_specs = (
        P("ja", "ka", None),
        P("ja", "ka", None),
        P(),
        P(),
        P(),
        P(),
        P(),
        P(),
        P(),
        P("ka", "ja", None),
    )
    out_specs = (P("ka", "ja", None), P("ja", "ka", None), P("ja", "ka", None))
    return jax.shard_map(shards, mesh=mesh, in_specs=in_specs, out_specs=out_specs, check_vma=False)
```
